1024 devices in a mesh: region: 128 (over z, y), mp: 8 (over x, core).
Axes of the slice: x: 4, y: 8, z: 16, core: 2. Of those that a mesh axis runs over, the one named last changes fastest.
Arguments:
- grid: bfloat16 [262144, 1024], P('region', 'mp'), may hold values from -6 to 6
- g2m_weight: float32 [262144], P('region'), may hold values from 0.3 to 1
- g2m_slot: int32 [262144], P('region'), may hold values from 0 to 511
- slot_node: int32 [128, 128, 4], P('region'), may hold values from 0 to 511, as said below
- peer_mask: int32 [128, 4], P('region'), may hold values 0 or 1
- norm_gain: float32 [1024], replicated, may hold values from 0.25 to 1.75
- w_qkv: bfloat16 [3, 1024, 1024], P(None, None, 'mp')
- w_out: bfloat16 [1024, 1024], P('mp'), may hold values from -0.1875 to 0.1875
Outputs:
- mesh_state: float32 [65536, 1024], P('region', 'mp')
- grid_out: bfloat16 [262144, 1024], P('region', 'mp')
The draws below stay inside these ranges and needn't reach their ends.
Inputs may be any that keep to these rules, and one draw needn't show every extreme that they name: `slot_node`: for each mesh tile o and lane c, the entries over all grid tiles r lie in one range b * (128) to (b + 1) * 128 - 1 and name every node of that range, where the range b depends on o and c and different lanes of one mesh tile take different ranges; so every mesh node is named by some send slot, and the 4 slots of one grid tile for one mesh tile name different nodes.
All inputs are finite; a program needn't handle non-finite values. No bound on the sum of `peer_mask` on one device may be relied on, other than what follows from the above.
Results may differ from the reference program's by a relative error of at most 0.006.
Values may be sent and summed in bfloat16 or wider, within the bound.
No kernel may reach another device: no remote copies, remote signals or barrier semaphores. Data moves between devices by JAX's collectives and lax.ppermute only.
A program may use at most 64 MiB of HBM per device.

```python
import math
import jax
import jax.numpy as jnp
from jax import lax

D = 1024
HEADS = 16
HEAD_DIM = 64
MESH_DEV = 512
GRID_DEV = 2048
SEND_SLOTS = 512
GRID = 262144
N_REGION = 128


def draw_slot_node(key, part):
    cap = SEND_SLOTS // N_REGION
    stride = MESH_DEV // cap
    keys = jax.random.split(jax.random.fold_in(key, 17), N_REGION * cap)
    orders = jax.vmap(lambda k: jax.random.permutation(k, N_REGION))(keys).astype(jnp.int32)
    orders = orders.reshape(N_REGION, cap, N_REGION)
    lane_keys = jax.random.split(jax.random.fold_in(key, 23), N_REGION)
    ranges = jax.vmap(lambda k: jax.random.permutation(k, cap))(lane_keys).astype(jnp.int32)
    table = orders % stride + ranges[:, :, None] * stride
    return jnp.transpose(table, (0, 2, 1)).astype(jnp.int32)


def draw_w_qkv(key, part):
    first = jax.random.fold_in(jax.random.fold_in(key, 29), 0)
    base = jax.random.normal(first, (3, D, D), jnp.float32) * D ** (-0.5)
    return base.astype(jnp.bfloat16)


def place_ends(array, own_key, least, largest):
    extent = array.shape
    place = [jax.random.randint(jax.random.fold_in(own_key, axis), (), 0, extent[axis]) for axis in range(len(extent))]
    array = array.at[tuple(place)].set(least)
    longest = extent.index(max(extent))
    place[longest] = (place[longest] + 1) % extent[longest]
    return array.at[tuple(place)].set(largest)


def shard_levels(rng, shape, cuts, least, top_value):
    def one(dim, parts):
        heights = jax.random.uniform(jax.random.fold_in(jax.random.fold_in(rng, 6), dim), (parts,), jnp.float32, least / len(cuts), top_value / len(cuts))
        return jnp.repeat(jnp.exp(heights), shape[dim] // parts).reshape((-1,) + (1,) * (len(shape) - dim - 1))

    loudness = one(*cuts[0])
    for cut in cuts[1:]:
        loudness = loudness * one(*cut)
    return loudness


def centred(stream_key, extent, scale, limit, pieces=(), kind=jnp.bfloat16):
    loudness = shard_levels(stream_key, extent, pieces, -0.22, 0.18) if pieces else 1.0
    entries = jax.random.normal(stream_key, extent, jnp.float32) * scale * loudness
    return jnp.minimum(jnp.maximum(entries, -limit), limit).astype(kind)


def setup_inputs(seed: int = 0) -> dict:
    streams_of = jax.random.split(jax.random.key(seed), 9)
    return {
        "grid": centred(streams_of[0], (GRID, D), 1.0, 6.0, ((0, 128), (1, 8))),
        "g2m_weight": jnp.clip(jnp.exp(math.log(1.0) - 1.2039728 * jax.random.uniform(streams_of[1], (GRID,), jnp.float32) ** shard_levels(streams_of[1], (GRID,), ((0, 128),), -0.2, 0.2)), 0.3, 1.0),
        "g2m_slot": place_ends(jax.random.randint(streams_of[2], (GRID,), 0, SEND_SLOTS), jax.random.fold_in(streams_of[2], 1), 0, SEND_SLOTS - 1).astype(jnp.int32),
        "slot_node": draw_slot_node(jax.random.fold_in(streams_of[8], 71), 0),
        "peer_mask": place_ends((jax.random.randint(streams_of[4], (N_REGION, 4), 0, 4) < 3).astype(jnp.int32), jax.random.fold_in(streams_of[4], 1), 0, 1),
        "norm_gain": jnp.clip(1.0 + 0.15 * jax.random.normal(streams_of[5], (D,), jnp.float32), 0.25, 1.75),
        "w_qkv": draw_w_qkv(jax.random.fold_in(streams_of[8], 71), 0),
        "w_out": centred(streams_of[7], (D, D), D ** -0.5, 0.1875, ((0, 8),)),
    }


OFFSETS = (-2, -1, 1, 2)

def reference(grid, g2m_weight, g2m_slot, slot_node, peer_mask, norm_gain, w_qkv, w_out):
    regions = N_REGION
    cap = SEND_SLOTS // N_REGION
    scaled = (g2m_weight[:, None] * grid.astype(jnp.float32)).astype(jnp.bfloat16)
    scaled = scaled.reshape(regions, GRID_DEV, D)
    slot_tiles = g2m_slot.reshape(regions, GRID_DEV).astype(jnp.int32)

    def tile_partial(pair):
        values, slots = pair
        onehot = (slots[None, :] == jnp.arange(SEND_SLOTS, dtype=jnp.int32)[:, None]).astype(jnp.bfloat16)
        return jnp.dot(onehot, values, preferred_element_type=jnp.float32).astype(jnp.bfloat16)
    partial_value = lax.map(tile_partial, (scaled, slot_tiles))
    owners = jnp.arange(SEND_SLOTS, dtype=jnp.int32) // cap
    by_grid = jnp.transpose(slot_node, (1, 0, 2)).reshape(regions, SEND_SLOTS).astype(jnp.int32)
    node_table = (owners[None, :] * MESH_DEV + by_grid).astype(jnp.int32)
    mesh_in = jax.ops.segment_sum(partial_value.reshape(-1, D).astype(jnp.float32), node_table.reshape(-1), num_segments=MESH_DEV * regions)
    mesh_low = lax.optimization_barrier(mesh_in.astype(jnp.bfloat16)).astype(jnp.float32)
    normed = (mesh_low * lax.rsqrt(lax.optimization_barrier(jnp.mean(mesh_low * mesh_low, axis=-1, keepdims=True)) + 1e-05) * norm_gain).astype(jnp.bfloat16)
    queries = jnp.dot(normed, w_qkv[0], preferred_element_type=jnp.float32).astype(jnp.bfloat16)
    keys = jnp.dot(normed, w_qkv[1], preferred_element_type=jnp.float32).astype(jnp.bfloat16)
    values = jnp.dot(normed, w_qkv[2], preferred_element_type=jnp.float32).astype(jnp.bfloat16)
    q_tiles = queries.reshape(regions, MESH_DEV, HEADS, HEAD_DIM)
    k_tiles = keys.reshape(regions, MESH_DEV, HEADS, HEAD_DIM)
    v_tiles = values.reshape(regions, MESH_DEV, HEADS, HEAD_DIM)

    def tile_attend(tile):
        order = [tile] + [(tile + offset) % regions for offset in OFFSETS]
        key_block = jnp.concatenate([k_tiles[index] for index in order], axis=0)
        val_block = jnp.concatenate([v_tiles[index] for index in order], axis=0)
        active = jnp.concatenate([jnp.ones((1,), jnp.int32), peer_mask[tile].astype(jnp.int32)])
        valid = jnp.repeat(active, MESH_DEV)
        scores = jnp.einsum('qhd,khd->hqk', q_tiles[tile].astype(jnp.float32), key_block.astype(jnp.float32)) * HEAD_DIM ** (-0.5)
        scores = jnp.where(valid[None, None, :] > 0, scores, -1e+30)
        top = lax.optimization_barrier(jnp.max(scores, axis=-1, keepdims=True))
        expd = jnp.exp(scores - top)
        weights = (expd / lax.optimization_barrier(jnp.sum(expd, axis=-1, keepdims=True))).astype(jnp.bfloat16)
        out = jnp.einsum('hqk,khd->qhd', weights.astype(jnp.float32), val_block.astype(jnp.float32))
        return out.astype(jnp.bfloat16).reshape(MESH_DEV, D)
    attended = lax.map(tile_attend, jnp.arange(regions, dtype=jnp.int32)).reshape(-1, D)
    mesh_state = mesh_in + jnp.dot(attended, w_out, preferred_element_type=jnp.float32)
    mesh_back = mesh_state.astype(jnp.bfloat16)
    point_nodes = jnp.take_along_axis(node_table, slot_tiles, axis=1).reshape(-1)
    grid_out = (grid.astype(jnp.float32) + mesh_back[point_nodes].astype(jnp.float32)).astype(jnp.bfloat16)
    return (mesh_state, grid_out)
```

```python
import jax
import jax.numpy as jnp
from jax import lax
from jax.experimental import pallas as pl
from jax.experimental.pallas import tpu as pltpu
from jax.sharding import Mesh
from jax.sharding import PartitionSpec as P

HEAD_DIM = 64
BF16 = jnp.bfloat16
F32 = jnp.float32
VMEM = pl.BlockSpec(memory_space=pltpu.VMEM)
SMEM = pl.BlockSpec(memory_space=pltpu.SMEM)
PARAMS = pltpu.CompilerParams(vmem_limit_bytes=32 * 1024 * 1024)


def exchange(array, axis):
    return lax.all_to_all(array, axis, split_axis=0, concat_axis=0, tiled=True)


def shifted(value, axis, steps):
    count = lax.axis_size(axis)
    pairs = [(source, (source + steps) % count) for source in range(count)]
    return lax.ppermute(value, axis, pairs)


def qkv_kernel(core_ref, own_ref, other_ref, gain_ref, w_ref, q_ref, kv_ref, normed_ref):
    core = core_ref[0]
    blocks, rows, width = own_ref.shape
    chunk = 128

    def normalise(step, _):
        at = pl.ds(pl.multiple_of(step * chunk, chunk), chunk)
        total = jnp.zeros((chunk, width), F32)
        for ref in (own_ref, other_ref):
            for block in range(blocks):
                value = ref[block, at, :].astype(F32)
                total = total + value * value
        mean = jnp.sum(total, axis=-1, keepdims=True) / (2 * blocks * width)
        factor = lax.rsqrt(mean + 1e-05)
        for ref, part in ((own_ref, core), (other_ref, 1 - core)):
            for block in range(blocks):
                index = 2 * block + part
                gain = gain_ref[pl.ds(index, 1), :]
                value = (ref[block, at, :].astype(F32) * factor * gain).astype(BF16)
                normed_ref[at, pl.ds(pl.multiple_of(index * width, width), width)] = value
        normed = normed_ref[at, :]
        queries = jnp.dot(normed, w_ref[0], preferred_element_type=F32).astype(BF16)
        q_ref[at, :] = queries
        kv_ref[at, :] = jnp.dot(normed, w_ref[1], preferred_element_type=F32).astype(BF16)
        later = pl.ds(pl.multiple_of(rows + step * chunk, chunk), chunk)
        kv_ref[later, :] = jnp.dot(normed, w_ref[2], preferred_element_type=F32).astype(BF16)
        return 0

    lax.fori_loop(0, rows // chunk, normalise, 0)


def attend_block(q_ref, kv_ref, top_ref, total_ref, mixed_ref, first):
    rows, width = q_ref.shape
    chunk = 256
    lane = lax.broadcasted_iota(jnp.int32, (1, width), 1)
    heads = width // HEAD_DIM
    keys = kv_ref[pl.ds(0, rows), :]
    values = kv_ref[pl.ds(rows, rows), :]
    for start in range(0, rows, chunk):
        at = pl.ds(start, chunk)
        queries = q_ref[at, :] * HEAD_DIM ** (-0.5)
        if first:
            tops, totals, mixed = None, None, None
        else:
            tops, totals, mixed = top_ref[at, :], total_ref[at, :], mixed_ref[at, :]
        new_tops = jnp.zeros((chunk, width), F32)
        expds = []
        for head in range(heads):
            mine = lane // HEAD_DIM == head
            scores = lax.dot_general(
                jnp.where(mine, queries, 0).astype(BF16),
                keys,
                (((1,), (1,)), ((), ())),
                preferred_element_type=F32,
            )
            top = jnp.max(scores, axis=-1, keepdims=True)
            if not first:
                top = jnp.maximum(top, tops[:, head * HEAD_DIM : head * HEAD_DIM + 1])
            expds.append(jnp.exp(scores - top).astype(BF16))
            new_tops = jnp.where(mine, top, new_tops)
        gained = jnp.zeros((chunk, 2 * width), F32)
        for head in range(heads):
            mine = lane // HEAD_DIM == head
            masked = jnp.where(mine, values, 0).astype(BF16)
            ones = jnp.broadcast_to(jnp.where(mine, 1.0, 0.0), values.shape).astype(BF16)
            gained = gained + jnp.dot(
                expds[head], jnp.concatenate([masked, ones], axis=1), preferred_element_type=F32
            )
        if first:
            mixed_ref[at, :] = gained[:, :width]
            total_ref[at, :] = gained[:, width:]
        else:
            shrink = jnp.exp(tops - new_tops)
            mixed_ref[at, :] = mixed * shrink + gained[:, :width]
            total_ref[at, :] = totals * shrink + gained[:, width:]
        top_ref[at, :] = new_tops


def own_kernel(q_ref, kv_ref, top_ref, total_ref, mixed_ref):
    attend_block(q_ref, kv_ref, top_ref, total_ref, mixed_ref, True)


def seen_blocks(mask_ref, picks, q_ref, kv_refs, top_ref, total_ref, mixed_ref):
    for pick, kv_ref in zip(picks, kv_refs):

        @pl.when(mask_ref[pick] > 0)
        def _(kv_ref=kv_ref):
            attend_block(q_ref, kv_ref, top_ref, total_ref, mixed_ref, False)


def near_kernel(
    mask_ref, q_ref, behind_ref, ahead_ref, top0_ref, total0_ref, mixed0_ref, top_ref, total_ref, mixed_ref
):
    top_ref[...] = top0_ref[...]
    total_ref[...] = total0_ref[...]
    mixed_ref[...] = mixed0_ref[...]
    seen_blocks(mask_ref, (1, 2), q_ref, (behind_ref, ahead_ref), top_ref, total_ref, mixed_ref)


def far_kernel(
    mask_ref,
    core_ref,
    q_ref,
    behind_ref,
    ahead_ref,
    top0_ref,
    total0_ref,
    mixed0_ref,
    w_ref,
    att_ref,
    out_ref,
    top_ref,
    total_ref,
    mixed_ref,
):
    top_ref[...] = top0_ref[...]
    total_ref[...] = total0_ref[...]
    mixed_ref[...] = mixed0_ref[...]
    seen_blocks(mask_ref, (0, 3), q_ref, (behind_ref, ahead_ref), top_ref, total_ref, mixed_ref)
    attended = (mixed_ref[...] / total_ref[...]).astype(BF16)
    att_ref[...] = attended
    blocks, _, width = out_ref.shape
    part = 1 - core_ref[0]
    for block in range(blocks):
        at = pl.ds(pl.multiple_of((2 * block + part) * width, width), width)
        out_ref[block] = jnp.dot(attended, w_ref[:, at], preferred_element_type=F32).astype(BF16)


def share_kernel(core_ref, att_ref, w_ref, arrived_ref, out_ref):
    blocks, _, width = out_ref.shape
    core = core_ref[0]
    for block in range(blocks):
        at = pl.ds(pl.multiple_of((2 * block + core) * width, width), width)
        share = jnp.dot(att_ref[...], w_ref[:, at], preferred_element_type=F32)
        out_ref[block] = (share + arrived_ref[block].astype(F32)).astype(BF16)


def call(kernel, outs, ins, name, scratch=(), flops=0, bytes_accessed=0, transcendentals=0):
    return pl.pallas_call(
        kernel,
        out_shape=outs,
        in_specs=ins,
        out_specs=jax.tree.map(lambda _: VMEM, outs),
        scratch_shapes=list(scratch),
        compiler_params=PARAMS,
        name=name,
        cost_estimate=pl.CostEstimate(
            flops=flops, bytes_accessed=bytes_accessed, transcendentals=transcendentals
        ),
    )


def on_device(grid, g2m_weight, g2m_slot, slot_node, peer_mask, norm_gain, w_qkv, w_out):
    regions = lax.axis_size("region")
    chips = lax.axis_size("x")
    cap = slot_node.shape[2]
    slots = regions * cap
    rows = slots
    width = grid.shape[1]
    core = lax.axis_index("core").astype(jnp.int32).reshape(1)
    sds = jax.ShapeDtypeStruct

    scaled = (g2m_weight[:, None] * grid.astype(F32)).astype(BF16)
    slot_hot = (g2m_slot[None, :] == jnp.arange(slots, dtype=jnp.int32)[:, None]).astype(BF16)
    partial_value = jnp.dot(slot_hot, scaled, preferred_element_type=F32).astype(BF16)
    mesh_low = exchange(partial_value.reshape(regions, cap, width), "region").reshape(rows, width)

    own = exchange(jnp.broadcast_to(mesh_low, (chips, rows, width)), "x")
    other = shifted(own, "core", 1)
    queries, kv = call(
        qkv_kernel,
        (sds((rows, width), BF16), sds((2 * rows, width), BF16)),
        [SMEM, VMEM, VMEM, VMEM, VMEM],
        "qkv",
        scratch=[pltpu.VMEM((rows, 2 * chips * width), BF16)],
        flops=2 * rows * 1024 * 384,
        bytes_accessed=3 << 20,
    )(core, own, other, norm_gain.reshape(2 * chips, width), w_qkv)

    state = sds((rows, width), F32)
    states = (state, state, state)
    mask = peer_mask.reshape(-1)
    block_cost = dict(flops=8 * rows * rows * width, transcendentals=2 * rows * rows)
    behind = shifted(kv, "region", 1)
    ahead = shifted(kv, "region", -1)
    top, total, mixed = call(own_kernel, states, [VMEM] * 2, "own", **block_cost)(queries, kv)
    behind2 = shifted(behind, "region", 1)
    ahead2 = shifted(ahead, "region", -1)
    twice = {key: 2 * value for key, value in block_cost.items()}
    top, total, mixed = call(near_kernel, states, [SMEM] + [VMEM] * 6, "near", **twice)(
        mask, queries, behind, ahead, top, total, mixed
    )
    shares = sds((chips, rows, width), BF16)
    attended, leaving = call(
        far_kernel,
        (sds((rows, width), BF16), shares),
        [SMEM, SMEM] + [VMEM] * 7,
        "far",
        scratch=[pltpu.VMEM((rows, width), F32)] * 3,
        **twice,
    )(mask, core, queries, behind2, ahead2, top, total, mixed, w_out)
    arrived = shifted(leaving, "core", 1)
    summed = call(share_kernel, shares, [SMEM] + [VMEM] * 3, "share")(core, attended, w_out, arrived)
    mesh_slots = mesh_low.astype(F32) + exchange(summed, "x").astype(F32).sum(axis=0)

    mesh_back = mesh_slots.astype(BF16)
    returned = exchange(mesh_back.reshape(regions, cap, width), "region").reshape(slots, width)
    flat_nodes = slot_node[0].reshape(-1)
    node_hot = (jnp.arange(rows, dtype=jnp.int32)[:, None] == flat_nodes[None, :]).astype(F32)
    mesh_state = jnp.dot(
        node_hot, mesh_slots, precision=lax.Precision.HIGHEST, preferred_element_type=F32
    )
    gathered = jnp.dot(slot_hot.T, returned, preferred_element_type=F32)
    grid_out = (grid.astype(F32) + gathered).astype(BF16)
    return (mesh_state, grid_out)


def solution(mesh):
    regions, model = mesh.devices.shape
    split = Mesh(mesh.devices.reshape(regions, model // 2, 2), ("region", "x", "core"))
    model = ("x", "core")
    return jax.shard_map(
        on_device,
        mesh=split,
        in_specs=(
            P("region", model),
            P("region"),
            P("region"),
            P("region", None, None),
            P("region", None),
            P(),
            P(None, None, model),
            P(model, None),
        ),
        out_specs=(P("region", model), P("region", model)),
        check_vma=False,
    )
```

```python
import jax
import jax.numpy as jnp
from jax import lax
from jax.experimental import pallas as pl
from jax.experimental.pallas import tpu as pltpu
from jax.sharding import Mesh
from jax.sharding import PartitionSpec as P

HEAD_DIM = 64
BF16 = jnp.bfloat16
F32 = jnp.float32
VMEM = pl.BlockSpec(memory_space=pltpu.VMEM)
SMEM = pl.BlockSpec(memory_space=pltpu.SMEM)
PARAMS = pltpu.CompilerParams(vmem_limit_bytes=32 * 1024 * 1024)


def exchange(array, axis):
    return lax.all_to_all(array, axis, split_axis=0, concat_axis=0, tiled=True)


def other_core(value):
    return lax.ppermute(value, "core", [(0, 1), (1, 0)])


def swapped(value, first):
    count = lax.axis_size("region")
    pairs = []
    for tile in range(count):
        ahead = (tile % 2 == 0) == first
        pairs.append((tile, (tile + (1 if ahead else -1)) % count))
    return lax.ppermute(value, "region", pairs)


def after(value, *earlier):
    return lax.optimization_barrier((value, *earlier))[0]


def half_product(part, x_ref, gain_ref, w_ref, scaled_ref, rows_ref, begin):
    blocks, rows, width = x_ref.shape
    for block in range(blocks):
        index = 2 * block + part
        at = pl.ds(block * width, width)
        source = pl.ds(pl.multiple_of(index * width, width), width)
        for third in range(3):
            rows_ref[at, third * width : (third + 1) * width] = w_ref[third, source, :]
    chunk = 128

    def step(i, _):
        at = pl.ds(pl.multiple_of(i * chunk, chunk), chunk)
        total = jnp.zeros((chunk, width), F32)
        for block in range(blocks):
            value = x_ref[block, at, :].astype(F32)
            total = total + value * value
            gain = gain_ref[pl.ds(2 * block + part, 1), :]
            scaled_ref[:, block * width : (block + 1) * width] = (value * gain).astype(BF16)
        square = jnp.sum(total, axis=-1, keepdims=True)
        begin(at, square, jnp.dot(scaled_ref[...], rows_ref[...], preferred_element_type=F32))
        return 0

    lax.fori_loop(0, rows // chunk, step, 0)


def own_half_kernel(core_ref, x_ref, gain_ref, w_ref, product_ref, square_ref, scaled_ref, rows_ref):
    def keep(at, square, product):
        product_ref[at, :] = product
        square_ref[at, :] = jnp.broadcast_to(square, (square.shape[0], square_ref.shape[1]))

    half_product(core_ref[0], x_ref, gain_ref, w_ref, scaled_ref, rows_ref, keep)


def other_half_kernel(
    core_ref, x_ref, gain_ref, w_ref, product_ref, square_ref, q_ref, kv_ref, scaled_ref, rows_ref
):
    blocks, rows, width = x_ref.shape

    def finish(at, square, product):
        mean = (square + square_ref[at, :]) / (2 * blocks * width)
        factor = lax.rsqrt(mean + 1e-05)
        for third in range(3):
            columns = slice(third * width, (third + 1) * width)
            whole = ((product[:, columns] + product_ref[at, columns]) * factor).astype(BF16)
            if third == 0:
                q_ref[at, :] = whole
            elif third == 1:
                kv_ref[at, :] = whole
            else:
                kv_ref[pl.ds(pl.multiple_of(rows + at.start, 128), at.size), :] = whole

    half_product(1 - core_ref[0], x_ref, gain_ref, w_ref, scaled_ref, rows_ref, finish)


def attend_block(q_ref, kv_ref, before, put):
    rows, width = q_ref.shape
    chunk = 256
    heads = width // HEAD_DIM
    lane = lax.broadcasted_iota(jnp.int32, (1, width), 1)
    keys = kv_ref[pl.ds(0, rows), :]
    values = kv_ref[pl.ds(rows, rows), :]
    summed = []
    for head in range(heads):
        mine = lane // HEAD_DIM == head
        ones = jnp.broadcast_to(jnp.where(mine, 1.0, 0.0), values.shape).astype(BF16)
        summed.append(jnp.concatenate([jnp.where(mine, values, 0).astype(BF16), ones], axis=1))
    for start in range(0, rows, chunk):
        at = pl.ds(start, chunk)
        queries = q_ref[at, :] * HEAD_DIM ** (-0.5)
        if before is not None:
            tops = before[0][at, :]
        new_tops = jnp.zeros((chunk, width), F32)
        gained = jnp.zeros((chunk, 2 * width), F32)
        for head in range(heads):
            mine = lane // HEAD_DIM == head
            scores = lax.dot_general(
                jnp.where(mine, queries, 0).astype(BF16),
                keys,
                (((1,), (1,)), ((), ())),
                preferred_element_type=F32,
            )
            top = jnp.max(scores, axis=-1, keepdims=True)
            if before is not None:
                top = jnp.maximum(top, tops[:, head * HEAD_DIM : head * HEAD_DIM + 1])
            expd = jnp.exp(scores - top).astype(BF16)
            gained = gained + jnp.dot(expd, summed[head], preferred_element_type=F32)
            new_tops = jnp.where(mine, top, new_tops)
        mixed, total = gained[:, :width], gained[:, width:]
        if before is not None:
            shrink = jnp.exp(tops - new_tops)
            mixed = before[2][at, :] * shrink + mixed
            total = before[1][at, :] * shrink + total
        put(at, new_tops, total, mixed)


def own_kernel(q_ref, kv_ref, top_ref, total_ref, mixed_ref):
    def put(at, top, total, mixed):
        top_ref[at, :] = top
        total_ref[at, :] = total
        mixed_ref[at, :] = mixed

    attend_block(q_ref, kv_ref, None, put)


PICKS = ((2, 1), (1, 2), (3, 0), (0, 3))


def is_seen(pick, mask_ref, odd_ref):
    even, odd = PICKS[pick]
    return mask_ref[0, jnp.where(odd_ref[0] == 0, even, odd)] > 0


def peer_kernel(
    pick, mask_ref, odd_ref, q_ref, kv_ref, top0_ref, total0_ref, mixed0_ref, top_ref, total_ref, mixed_ref
):
    before = (top0_ref, total0_ref, mixed0_ref)
    seen = is_seen(pick, mask_ref, odd_ref)

    def put(at, top, total, mixed):
        top_ref[at, :] = top
        total_ref[at, :] = total
        mixed_ref[at, :] = mixed

    @pl.when(seen)
    def _():
        attend_block(q_ref, kv_ref, before, put)

    @pl.when(jnp.logical_not(seen))
    def _():
        for old_ref, new_ref in zip(before, (top_ref, total_ref, mixed_ref)):
            new_ref[...] = old_ref[...]


def last_kernel(pick, mask_ref, odd_ref, q_ref, kv_ref, top0_ref, total0_ref, mixed0_ref, att_ref):
    before = (top0_ref, total0_ref, mixed0_ref)
    seen = is_seen(pick, mask_ref, odd_ref)

    def put(at, top, total, mixed):
        att_ref[at, :] = (mixed / total).astype(BF16)

    @pl.when(seen)
    def _():
        attend_block(q_ref, kv_ref, before, put)

    @pl.when(jnp.logical_not(seen))
    def _():
        att_ref[...] = (mixed0_ref[...] / total0_ref[...]).astype(BF16)


def share_kernel(core_ref, own_ref, other_ref, w_own_ref, w_other_ref, out_ref):
    blocks, _, width = out_ref.shape
    core = core_ref[0]
    both = jnp.concatenate([own_ref[...], other_ref[...]], axis=1)
    for block in range(blocks):
        at = pl.ds(pl.multiple_of((2 * block + core) * width, width), width)
        weight = jnp.concatenate([w_own_ref[:, at], w_other_ref[:, at]], axis=0)
        out_ref[block] = jnp.dot(both, weight, preferred_element_type=F32).astype(BF16)


def sum_kernel(base_ref, parts_ref, state_ref, back_ref):
    total = base_ref[...].astype(F32)
    for block in range(parts_ref.shape[0]):
        total = total + parts_ref[block].astype(F32)
    state_ref[...] = total
    back_ref[...] = total.astype(BF16)


def call(kernel, outs, scalars, arrays, name, scratch=(), flops=0, bytes_accessed=0, transcendentals=0):
    return pl.pallas_call(
        kernel,
        out_shape=outs,
        in_specs=[SMEM] * scalars + [VMEM] * arrays,
        out_specs=jax.tree.map(lambda _: VMEM, outs),
        scratch_shapes=list(scratch),
        compiler_params=PARAMS,
        name=name,
        cost_estimate=pl.CostEstimate(
            flops=flops, bytes_accessed=bytes_accessed, transcendentals=transcendentals
        ),
    )


def on_device(grid, g2m_weight, g2m_slot, slot_node, peer_mask, norm_gain, w_qkv, w_out):
    regions = lax.axis_size("region")
    chips = lax.axis_size("x")
    cap = slot_node.shape[2]
    slots = regions * cap
    rows = slots
    width = grid.shape[1]
    core = lax.axis_index("core").astype(jnp.int32).reshape(1)
    odd = (lax.axis_index("region") & 1).astype(jnp.int32).reshape(1)
    sds = jax.ShapeDtypeStruct

    scaled = (g2m_weight[:, None] * grid.astype(F32)).astype(BF16)
    slot_hot = (g2m_slot[None, :] == jnp.arange(slots, dtype=jnp.int32)[:, None]).astype(BF16)
    partial_value = jnp.dot(slot_hot, scaled, preferred_element_type=F32).astype(BF16)
    mesh_low = exchange(partial_value.reshape(regions, cap, width), "region").reshape(rows, width)

    own = exchange(jnp.broadcast_to(mesh_low, (chips, rows, width)), "x")
    other = other_core(own)
    gain = norm_gain.reshape(2 * chips, width)
    half = chips * width
    scratch = [pltpu.VMEM((128, half), BF16), pltpu.VMEM((half, 3 * width), BF16)]
    cost = dict(flops=2 * rows * half * 3 * width, bytes_accessed=2 << 20)
    product, square = call(
        own_half_kernel,
        (sds((rows, 3 * width), F32), sds((rows, width), F32)),
        1,
        3,
        "own_half",
        scratch,
        **cost,
    )(core, own, gain, w_qkv)
    queries, kv = call(
        other_half_kernel,
        (sds((rows, width), BF16), sds((2 * rows, width), BF16)),
        1,
        5,
        "other_half",
        scratch,
        **cost,
    )(core, other, gain, w_qkv, product, square)

    state = sds((rows, width), F32)
    states = (state, state, state)
    cost = dict(flops=8 * rows * rows * width, transcendentals=2 * rows * rows)

    def peer(pick, block, so_far):
        def kernel(*refs):
            peer_kernel(pick, *refs)

        return call(kernel, states, 2, 5, f"peer{pick}", **cost)(
            peer_mask, odd, queries, block, *so_far
        )

    def last(*refs):
        last_kernel(2, *refs)

    near1 = swapped(kv, True)
    near2 = swapped(kv, False)
    so_far = call(own_kernel, states, 0, 2, "own", **cost)(queries, kv)
    far2 = swapped(after(near1, so_far[0]), False)
    far1 = swapped(near2, True)
    w_other = other_core(after(w_out, so_far[0]))
    so_far = peer(0, near1, so_far)
    so_far = peer(1, near2, (after(so_far[0], w_other), *so_far[1:]))
    so_far = peer(3, far2, so_far)
    attended = call(last, sds((rows, width), BF16), 2, 5, "last", **cost)(
        peer_mask, odd, queries, far1, *so_far
    )

    attended_other = other_core(attended)
    summed = call(
        share_kernel,
        sds((chips, rows, width), BF16),
        1,
        4,
        "share",
        flops=2 * rows * 2 * width * half,
    )(core, attended, attended_other, w_out, w_other)
    mesh_slots, mesh_back = call(
        sum_kernel, (state, sds((rows, width), BF16)), 0, 2, "sum", bytes_accessed=1 << 20
    )(mesh_low, exchange(summed, "x"))

    returned = exchange(mesh_back.reshape(regions, cap, width), "region").reshape(slots, width)
    flat_nodes = slot_node[0].reshape(-1)
    node_hot = (jnp.arange(rows, dtype=jnp.int32)[:, None] == flat_nodes[None, :]).astype(F32)
    mesh_state = jnp.dot(
        node_hot, mesh_slots, precision=lax.Precision.HIGHEST, preferred_element_type=F32
    )
    gathered = jnp.dot(slot_hot.T, returned, preferred_element_type=F32)
    grid_out = (grid.astype(F32) + gathered).astype(BF16)
    return (mesh_state, grid_out)


def solution(mesh):
    regions, model = mesh.devices.shape
    split = Mesh(mesh.devices.reshape(regions, model // 2, 2), ("region", "x", "core"))
    model = ("x", "core")
    return jax.shard_map(
        on_device,
        mesh=split,
        in_specs=(
            P("region", model),
            P("region"),
            P("region"),
            P("region", None, None),
            P("region", None),
            P(),
            P(None, None, model),
            P(model, None),
        ),
        out_specs=(P("region", model), P("region", model)),
        check_vma=False,
    )
```

```python
import jax
import jax.numpy as jnp
from jax import lax
from jax.experimental import pallas as pl
from jax.experimental.pallas import tpu as pltpu
from jax.sharding import Mesh
from jax.sharding import PartitionSpec as P

HEAD_DIM = 64
OFFSETS = (-2, -1, 1, 2)
CHUNK = 128
BF16 = jnp.bfloat16
F32 = jnp.float32
VMEM = pl.BlockSpec(memory_space=pltpu.VMEM)
PARAMS = pltpu.CompilerParams(vmem_limit_bytes=32 * 1024 * 1024)


def exchange(array, axis):
    return lax.all_to_all(array, axis, split_axis=0, concat_axis=0, tiled=True)


def other_core(value):
    return lax.ppermute(value, "core", [(0, 1), (1, 0)])


def swapped(value, axis, first):
    count, cores = lax.axis_size(axis), lax.axis_size("core")
    pairs = []
    for place in range(count):
        for core in range(cores):
            ahead = ((place + core) % 2 == 0) == first
            partner = (place + (1 if ahead else -1)) % count
            pairs.append((place * cores + core, partner * cores + core))
    return lax.ppermute(value, (axis, "core"), pairs)


def after(value, *earlier):
    return lax.optimization_barrier((value, *earlier))[0]


def feature_places():
    core, chip, chips = lax.axis_index("core"), lax.axis_index("x"), lax.axis_size("x")
    step = 1 - 2 * ((chip + core) & 1)
    wrap = lambda place: lax.rem(place + chips, chips)
    return core, (chip, wrap(chip + step), wrap(chip - step), wrap(chip + 2))


def block_product(blocks, gain_ref, w_ref, scaled_ref, rows_ref, put):
    rows, width = blocks[0][0].shape
    for i, (_, index) in enumerate(blocks):
        source = pl.ds(pl.multiple_of(index * width, width), width)
        for third in range(3):
            columns = slice(third * width, (third + 1) * width)
            rows_ref[i * width : (i + 1) * width, columns] = w_ref[third, source, :]

    def step(number, _):
        at = pl.ds(pl.multiple_of(number * CHUNK, CHUNK), CHUNK)
        total = jnp.zeros((CHUNK, width), F32)
        for i, (ref, index) in enumerate(blocks):
            value = ref[at, :].astype(F32)
            total = total + value * value
            gain = gain_ref[pl.ds(index, 1), :]
            scaled_ref[:, i * width : (i + 1) * width] = (value * gain).astype(BF16)
        put(at, total, jnp.dot(scaled_ref[...], rows_ref[...], preferred_element_type=F32))
        return 0

    lax.fori_loop(0, rows // CHUNK, step, 0)


def early_kernel(
    own_ref, first_ref, second_ref, gain_ref, w_ref, w_out_ref, square_ref, product_ref, sent_ref, *scratch
):
    core, (own, first, second, _) = feature_places()
    rows, width = own_ref.shape
    for i, ref in enumerate((own_ref, first_ref, second_ref)):
        sent_ref[i * rows : (i + 1) * rows, :] = ref[...]
    for i in range(gain_ref.shape[0]):
        sent_ref[4 * rows + i * width : 4 * rows + (i + 1) * width, :] = w_out_ref[:, i * width : (i + 1) * width]

    def put(at, square, product):
        square_ref[at, :] = square
        product_ref[at, :] = product

    blocks = [(own_ref, 2 * own + core), (first_ref, 2 * first + core), (second_ref, 2 * second + core)]
    block_product(blocks, gain_ref, w_ref, *scratch, put)


def middle_kernel(last_ref, gain_ref, w_ref, square0_ref, product0_ref, square_ref, product_ref, *scratch):
    core, (_, _, _, last) = feature_places()

    def put(at, square, product):
        square_ref[at, :] = square0_ref[at, :] + square
        product_ref[at, :] = product0_ref[at, :] + product

    block_product([(last_ref, 2 * last + core)], gain_ref, w_ref, *scratch, put)


def late_kernel(arrived_ref, gain_ref, w_ref, square0_ref, product0_ref, q_ref, kv_ref, *scratch):
    core, (own, first, second, last) = feature_places()
    rows, width = q_ref.shape
    features = gain_ref.shape[0] * width

    def put(at, square, product):
        mean = jnp.sum(square0_ref[at, :] + square, axis=-1, keepdims=True) / features
        factor = lax.rsqrt(mean + 1e-05)
        whole = ((product0_ref[at, :] + product) * factor).astype(BF16)
        q_ref[at, :] = whole[:, :width]
        kv_ref[at, :] = whole[:, width : 2 * width]
        kv_ref[pl.ds(pl.multiple_of(rows + at.start, CHUNK), CHUNK), :] = whole[:, 2 * width :]

    blocks = []
    for i, chip in enumerate((own, second, first, last)):
        blocks.append((arrived_ref.at[pl.ds(i * rows, rows)], 2 * chip + 1 - core))
    block_product(blocks, gain_ref, w_ref, *scratch, put)


def attend_block(q_ref, kv_ref, seen, before, put):
    rows, width = q_ref.shape
    chunk = 256
    heads = width // HEAD_DIM
    lane = lax.broadcasted_iota(jnp.int32, (1, width), 1)
    keys = kv_ref[pl.ds(0, rows), :]
    values = kv_ref[pl.ds(rows, rows), :]
    summed = []
    for head in range(heads):
        mine = lane // HEAD_DIM == head
        ones = jnp.broadcast_to(jnp.where(mine, 1.0, 0.0), values.shape).astype(BF16)
        summed.append(jnp.concatenate([jnp.where(mine, values, 0).astype(BF16), ones], axis=1))
    for start in range(0, rows, chunk):
        at = pl.ds(start, chunk)
        queries = q_ref[at, :] * HEAD_DIM ** (-0.5)
        if before is not None:
            tops = before[0][at, :]
        new_tops = jnp.zeros((chunk, width), F32)
        gained = jnp.zeros((chunk, 2 * width), F32)
        for head in range(heads):
            mine = lane // HEAD_DIM == head
            scores = lax.dot_general(
                jnp.where(mine, queries, 0).astype(BF16),
                keys,
                (((1,), (1,)), ((), ())),
                preferred_element_type=F32,
            )
            if seen is not None:
                scores = jnp.where(seen, scores, -1e30)
            top = jnp.max(scores, axis=-1, keepdims=True)
            if before is not None:
                top = jnp.maximum(top, tops[:, head * HEAD_DIM : head * HEAD_DIM + 1])
            expd = jnp.exp(scores - top).astype(BF16)
            gained = gained + jnp.dot(expd, summed[head], preferred_element_type=F32)
            new_tops = jnp.where(mine, top, new_tops)
        mixed, total = gained[:, :width], gained[:, width:]
        if before is not None:
            shrink = jnp.exp(tops - new_tops)
            mixed = before[2][at, :] * shrink + mixed
            total = before[1][at, :] * shrink + total
        put(at, new_tops, total, mixed)


def is_seen(turn, mask_ref):
    odd = (lax.axis_index("region") + lax.axis_index("core")) & 1
    offset = (1, -1, -2, 2)[turn]
    wanted = jnp.where(odd == 0, OFFSETS.index(offset), OFFSETS.index(-offset))
    mask = mask_ref[...]
    lane = lax.broadcasted_iota(jnp.int32, mask.shape, 1)
    return jnp.sum(jnp.where(lane == wanted, mask, 0), axis=-1, keepdims=True) > 0


def own_kernel(q_ref, kv_ref, *states):
    def put(at, *values):
        for ref, value in zip(states, values):
            ref[at, :] = value

    attend_block(q_ref, kv_ref, None, None, put)


def peer_kernel(turn, mask_ref, q_ref, kv_ref, *states):
    def put(at, *values):
        for ref, value in zip(states[3:], values):
            ref[at, :] = value

    attend_block(q_ref, kv_ref, is_seen(turn, mask_ref), states[:3], put)


def last_kernel(turn, mask_ref, q_ref, kv_ref, *refs):
    def put(at, top, total, mixed):
        refs[3][at, :] = (mixed / total).astype(BF16)

    attend_block(q_ref, kv_ref, is_seen(turn, mask_ref), refs[:3], put)


def column_share(chip, core, own_ref, other_ref, w_own_ref, arrived_ref):
    rows, width = own_ref.shape
    index = 2 * chip + core
    at = pl.ds(pl.multiple_of(index * width, width), width)
    both = jnp.concatenate([own_ref[...], other_ref[...]], axis=1)
    w_other = arrived_ref[pl.ds(pl.multiple_of(4 * rows + index * width, width), width), :]
    weight = jnp.concatenate([w_own_ref[:, at], w_other], axis=0)
    return jnp.dot(both, weight, preferred_element_type=F32)


def far_share_kernel(*refs):
    core, (_, _, _, last) = feature_places()
    refs[4][...] = column_share(last, core, *refs[:4]).astype(BF16)


def near_share_kernel(*refs):
    core, (own, first, second, _) = feature_places()
    ins, (base_ref, own_out, first_out, second_out) = refs[:4], refs[4:]
    second_out[...] = column_share(second, core, *ins).astype(BF16)
    first_out[...] = column_share(first, core, *ins)
    own_out[...] = base_ref[...].astype(F32) + column_share(own, core, *ins)


def add_kernel(share_ref, arrived_ref, out_ref):
    out_ref[...] = (share_ref[...] + arrived_ref[...].astype(F32)).astype(BF16)


def sum_kernel(base_ref, first_ref, second_ref, state_ref, back_ref):
    total = base_ref[...] + (first_ref[...].astype(F32) + second_ref[...].astype(F32))
    state_ref[...] = total
    back_ref[...] = total.astype(BF16)


def call(kernel, outs, name, scratch=(), flops=0, bytes_accessed=0, transcendentals=0):
    def run(*args):
        return pl.pallas_call(
            kernel,
            out_shape=outs,
            in_specs=[VMEM] * len(args),
            out_specs=jax.tree.map(lambda _: VMEM, outs),
            scratch_shapes=list(scratch),
            compiler_params=PARAMS,
            name=name,
            cost_estimate=pl.CostEstimate(
                flops=flops, bytes_accessed=bytes_accessed, transcendentals=transcendentals
            ),
        )(*args)

    return run


def on_device(grid, g2m_weight, g2m_slot, slot_node, peer_mask, norm_gain, w_qkv, w_out):
    regions = lax.axis_size("region")
    parts = lax.axis_size("x") * lax.axis_size("core")
    cap = slot_node.shape[2]
    slots = regions * cap
    rows = slots
    width = grid.shape[1]
    low = jax.ShapeDtypeStruct((rows, width), BF16)
    state = jax.ShapeDtypeStruct((rows, width), F32)

    scaled = (g2m_weight[:, None] * grid.astype(F32)).astype(BF16)
    slot_hot = (g2m_slot[None, :] == jnp.arange(slots, dtype=jnp.int32)[:, None]).astype(BF16)
    partial_value = jnp.dot(slot_hot, scaled, preferred_element_type=F32).astype(BF16)
    mesh_low = exchange(partial_value.reshape(regions, cap, width), "region").reshape(rows, width)

    first = swapped(mesh_low, "x", True)
    second = swapped(mesh_low, "x", False)
    last = swapped(first, "x", False)
    gain = norm_gain.reshape(parts, width)

    def product(kernel, outs, name, blocks, *args):
        depth = blocks * width
        return call(
            kernel,
            outs,
            name,
            scratch=[pltpu.VMEM((CHUNK, depth), BF16), pltpu.VMEM((depth, 3 * width), BF16)],
            flops=6 * rows * depth * width,
            bytes_accessed=2 << 20,
        )(*args)

    sums = (state, jax.ShapeDtypeStruct((rows, 3 * width), F32))
    sent = jax.ShapeDtypeStruct((4 * rows + parts * width, width), BF16)
    *so_far, sent = product(
        early_kernel, (*sums, sent), "early", 3, mesh_low, first, second, gain, w_qkv, w_out
    )
    arrived = other_core(lax.dynamic_update_slice(sent, last, (3 * rows, 0)))
    so_far = product(middle_kernel, sums, "middle", 1, last, gain, w_qkv, *so_far)
    kvs = jax.ShapeDtypeStruct((2 * rows, width), BF16)
    queries, kv = product(late_kernel, (low, kvs), "late", 4, arrived, gain, w_qkv, *so_far)

    cost = dict(flops=8 * rows * rows * width, transcendentals=2 * rows * rows)

    def attend(turn, *args):
        outs, kernel = (low, last_kernel) if turn == 3 else ((state,) * 3, peer_kernel)
        return call(lambda *refs: kernel(turn, *refs), outs, f"peer{turn}", **cost)(
            peer_mask, queries, *args
        )

    kv0 = swapped(kv, "region", True)
    kv1 = swapped(kv, "region", False)
    so_far = call(own_kernel, (state,) * 3, "own", **cost)(queries, kv)
    kv2 = swapped(after(kv0, so_far[0]), "region", False)
    kv3 = swapped(kv1, "region", True)
    so_far = attend(0, kv0, *so_far)
    so_far = attend(1, kv1, *so_far)
    so_far = attend(2, kv2, *so_far)
    attended = attend(3, kv3, *so_far)

    shared = (attended, other_core(attended), w_out, arrived)
    flops = 4 * rows * width * width
    far_share = call(far_share_kernel, low, "far_share", flops=flops)(*shared)
    relayed = swapped(far_share, "x", False)
    base, first_share, second_share = call(
        near_share_kernel, (state, state, low), "near_share", flops=3 * flops
    )(*shared, mesh_low)
    from_second = swapped(second_share, "x", False)
    passed_on = call(add_kernel, low, "add", bytes_accessed=1 << 19)(first_share, relayed)
    from_first = swapped(passed_on, "x", True)
    mesh_slots, mesh_back = call(sum_kernel, (state, low), "sum", bytes_accessed=1 << 20)(
        base, from_first, from_second
    )

    returned = exchange(mesh_back.reshape(regions, cap, width), "region").reshape(slots, width)
    flat_nodes = slot_node[0].reshape(-1)
    node_hot = (jnp.arange(rows, dtype=jnp.int32)[:, None] == flat_nodes[None, :]).astype(F32)
    mesh_state = jnp.dot(
        node_hot, mesh_slots, precision=lax.Precision.HIGHEST, preferred_element_type=F32
    )
    gathered = jnp.dot(slot_hot.T, returned, preferred_element_type=F32)
    grid_out = (grid.astype(F32) + gathered).astype(BF16)
    return (mesh_state, grid_out)


def solution(mesh):
    regions, model = mesh.devices.shape
    split = Mesh(mesh.devices.reshape(regions, model // 2, 2), ("region", "x", "core"))
    model = ("x", "core")
    return jax.shard_map(
        on_device,
        mesh=split,
        in_specs=(
            P("region", model),
            P("region"),
            P("region"),
            P("region", None, None),
            P("region", None),
            P(),
            P(None, None, model),
            P(model, None),
        ),
        out_specs=(P("region", model), P("region", model)),
        check_vma=False,
    )
```

```python
import jax
import jax.numpy as jnp
from jax import lax
from jax.experimental import pallas as pl
from jax.experimental.pallas import tpu as pltpu
from jax.sharding import Mesh
from jax.sharding import PartitionSpec as P

HEAD_DIM = 64
OFFSETS = (-2, -1, 1, 2)
CHUNK = 128
BF16 = jnp.bfloat16
F32 = jnp.float32
VMEM = pl.BlockSpec(memory_space=pltpu.VMEM)
PARAMS = pltpu.CompilerParams(vmem_limit_bytes=32 * 1024 * 1024)


def exchange(array, axis):
    return lax.all_to_all(array, axis, split_axis=0, concat_axis=0, tiled=True)


def other_core(value):
    return lax.ppermute(value, "core", [(0, 1), (1, 0)])


def swapped(value, axis, first):
    count, cores = lax.axis_size(axis), lax.axis_size("core")
    pairs = []
    for place in range(count):
        for core in range(cores):
            ahead = ((place + core) % 2 == 0) == first
            partner = (place + (1 if ahead else -1)) % count
            pairs.append((place * cores + core, partner * cores + core))
    return lax.ppermute(value, (axis, "core"), pairs)


def after(value, *earlier):
    return lax.optimization_barrier((value, *earlier))[0]


def block_product(blocks, gain_ref, w_ref, scaled_ref, rows_ref, put):
    rows, width = blocks[0][0].shape
    for i, (_, index) in enumerate(blocks):
        source = pl.ds(pl.multiple_of(index * width, width), width)
        for third in range(3):
            columns = slice(third * width, (third + 1) * width)
            rows_ref[i * width : (i + 1) * width, columns] = w_ref[third, source, :]

    def step(number, _):
        at = pl.ds(pl.multiple_of(number * CHUNK, CHUNK), CHUNK)
        total = jnp.zeros((CHUNK, width), F32)
        for i, (ref, index) in enumerate(blocks):
            value = ref[at, :].astype(F32)
            total = total + value * value
            gain = gain_ref[pl.ds(index, 1), :]
            scaled_ref[:, i * width : (i + 1) * width] = (value * gain).astype(BF16)
        put(at, total, jnp.dot(scaled_ref[...], rows_ref[...], preferred_element_type=F32))
        return 0

    lax.fori_loop(0, rows // CHUNK, step, 0)


def own_half_kernel(own_ref, gain_ref, w_ref, square_ref, product_ref, *scratch):
    core = lax.axis_index("core")

    def put(at, square, product):
        square_ref[at, :] = square
        product_ref[at, :] = product

    blocks = [(own_ref.at[chip], 2 * chip + core) for chip in range(own_ref.shape[0])]
    block_product(blocks, gain_ref, w_ref, *scratch, put)


def other_half_kernel(other_ref, gain_ref, w_ref, square0_ref, product0_ref, q_ref, kv_ref, *scratch):
    core = lax.axis_index("core")
    rows, width = q_ref.shape
    features = gain_ref.shape[0] * width

    def put(at, square, product):
        mean = jnp.sum(square0_ref[at, :] + square, axis=-1, keepdims=True) / features
        factor = lax.rsqrt(mean + 1e-05)
        whole = ((product0_ref[at, :] + product) * factor).astype(BF16)
        q_ref[at, :] = whole[:, :width]
        kv_ref[at, :] = whole[:, width : 2 * width]
        kv_ref[pl.ds(pl.multiple_of(rows + at.start, CHUNK), CHUNK), :] = whole[:, 2 * width :]

    blocks = [(other_ref.at[chip], 2 * chip + 1 - core) for chip in range(other_ref.shape[0])]
    block_product(blocks, gain_ref, w_ref, *scratch, put)


def attend_block(q_ref, kv_ref, seen, before, put):
    rows, width = q_ref.shape
    chunk = 256
    heads = width // HEAD_DIM
    lane = lax.broadcasted_iota(jnp.int32, (1, width), 1)
    keys = kv_ref[pl.ds(0, rows), :]
    values = kv_ref[pl.ds(rows, rows), :]
    summed = []
    for head in range(heads):
        mine = lane // HEAD_DIM == head
        ones = jnp.broadcast_to(jnp.where(mine, 1.0, 0.0), values.shape).astype(BF16)
        summed.append(jnp.concatenate([jnp.where(mine, values, 0).astype(BF16), ones], axis=1))
    for start in range(0, rows, chunk):
        at = pl.ds(start, chunk)
        queries = q_ref[at, :] * HEAD_DIM ** (-0.5)
        if before is not None:
            tops = before[0][at, :]
        new_tops = jnp.zeros((chunk, width), F32)
        gained = jnp.zeros((chunk, 2 * width), F32)
        for head in range(heads):
            mine = lane // HEAD_DIM == head
            scores = lax.dot_general(
                jnp.where(mine, queries, 0).astype(BF16),
                keys,
                (((1,), (1,)), ((), ())),
                preferred_element_type=F32,
            )
            if seen is not None:
                scores = jnp.where(seen, scores, -1e30)
            top = jnp.max(scores, axis=-1, keepdims=True)
            if before is not None:
                top = jnp.maximum(top, tops[:, head * HEAD_DIM : head * HEAD_DIM + 1])
            expd = jnp.exp(scores - top).astype(BF16)
            gained = gained + jnp.dot(expd, summed[head], preferred_element_type=F32)
            new_tops = jnp.where(mine, top, new_tops)
        mixed, total = gained[:, :width], gained[:, width:]
        if before is not None:
            shrink = jnp.exp(tops - new_tops)
            mixed = before[2][at, :] * shrink + mixed
            total = before[1][at, :] * shrink + total
        put(at, new_tops, total, mixed)


def is_seen(turn, mask_ref):
    odd = (lax.axis_index("region") + lax.axis_index("core")) & 1
    offset = (1, -1, -2, 2)[turn]
    wanted = jnp.where(odd == 0, OFFSETS.index(offset), OFFSETS.index(-offset))
    mask = mask_ref[...]
    lane = lax.broadcasted_iota(jnp.int32, mask.shape, 1)
    return jnp.sum(jnp.where(lane == wanted, mask, 0), axis=-1, keepdims=True) > 0


def own_kernel(q_ref, kv_ref, *states):
    def put(at, *values):
        for ref, value in zip(states, values):
            ref[at, :] = value

    attend_block(q_ref, kv_ref, None, None, put)


def peer_kernel(turn, mask_ref, q_ref, kv_ref, *states):
    def put(at, *values):
        for ref, value in zip(states[3:], values):
            ref[at, :] = value

    attend_block(q_ref, kv_ref, is_seen(turn, mask_ref), states[:3], put)


def last_kernel(turn, mask_ref, q_ref, kv_ref, *refs):
    def put(at, top, total, mixed):
        refs[3][at, :] = (mixed / total).astype(BF16)

    attend_block(q_ref, kv_ref, is_seen(turn, mask_ref), refs[:3], put)


def share_kernel(own_ref, other_ref, w_own_ref, w_other_ref, out_ref):
    blocks, _, width = out_ref.shape
    core = lax.axis_index("core")
    both = jnp.concatenate([own_ref[...], other_ref[...]], axis=1)
    for block in range(blocks):
        at = pl.ds(pl.multiple_of((2 * block + core) * width, width), width)
        weight = jnp.concatenate([w_own_ref[:, at], w_other_ref[:, at]], axis=0)
        out_ref[block] = jnp.dot(both, weight, preferred_element_type=F32).astype(BF16)


def sum_kernel(base_ref, parts_ref, state_ref, back_ref):
    total = base_ref[...].astype(F32)
    for block in range(parts_ref.shape[0]):
        total = total + parts_ref[block].astype(F32)
    state_ref[...] = total
    back_ref[...] = total.astype(BF16)


def call(kernel, outs, name, scratch=(), flops=0, bytes_accessed=0, transcendentals=0):
    def run(*args):
        return pl.pallas_call(
            kernel,
            out_shape=outs,
            in_specs=[VMEM] * len(args),
            out_specs=jax.tree.map(lambda _: VMEM, outs),
            scratch_shapes=list(scratch),
            compiler_params=PARAMS,
            name=name,
            cost_estimate=pl.CostEstimate(
                flops=flops, bytes_accessed=bytes_accessed, transcendentals=transcendentals
            ),
        )(*args)

    return run


def on_device(grid, g2m_weight, g2m_slot, slot_node, peer_mask, norm_gain, w_qkv, w_out):
    regions = lax.axis_size("region")
    chips = lax.axis_size("x")
    parts = chips * lax.axis_size("core")
    cap = slot_node.shape[2]
    slots = regions * cap
    rows = slots
    width = grid.shape[1]
    low = jax.ShapeDtypeStruct((rows, width), BF16)
    state = jax.ShapeDtypeStruct((rows, width), F32)

    scaled = (g2m_weight[:, None] * grid.astype(F32)).astype(BF16)
    slot_hot = (g2m_slot[None, :] == jnp.arange(slots, dtype=jnp.int32)[:, None]).astype(BF16)
    partial_value = jnp.dot(slot_hot, scaled, preferred_element_type=F32).astype(BF16)
    mesh_low = exchange(partial_value.reshape(regions, cap, width), "region").reshape(rows, width)

    own = exchange(jnp.broadcast_to(mesh_low, (chips, rows, width)), "x")
    other = other_core(own)
    gain = norm_gain.reshape(parts, width)

    def product(kernel, outs, name, blocks, *args):
        depth = blocks * width
        return call(
            kernel,
            outs,
            name,
            scratch=[pltpu.VMEM((CHUNK, depth), BF16), pltpu.VMEM((depth, 3 * width), BF16)],
            flops=6 * rows * depth * width,
            bytes_accessed=2 << 20,
        )(*args)

    sums = (state, jax.ShapeDtypeStruct((rows, 3 * width), F32))
    kvs = jax.ShapeDtypeStruct((2 * rows, width), BF16)
    so_far = product(own_half_kernel, sums, "own_half", chips, own, gain, w_qkv)
    queries, kv = product(other_half_kernel, (low, kvs), "other_half", chips, other, gain, w_qkv, *so_far)

    cost = dict(flops=8 * rows * rows * width, transcendentals=2 * rows * rows)

    def attend(turn, *args):
        outs, kernel = (low, last_kernel) if turn == 3 else ((state,) * 3, peer_kernel)
        return call(lambda *refs: kernel(turn, *refs), outs, f"peer{turn}", **cost)(
            peer_mask, queries, *args
        )

    kv0 = swapped(kv, "region", True)
    kv1 = swapped(kv, "region", False)
    so_far = call(own_kernel, (state,) * 3, "own", **cost)(queries, kv)
    kv2 = swapped(after(kv0, so_far[0]), "region", False)
    kv3 = swapped(kv1, "region", True)
    w_other = other_core(after(w_out, so_far[0]))
    so_far = attend(0, kv0, *so_far)
    so_far = attend(1, kv1, after(so_far[0], w_other), *so_far[1:])
    so_far = attend(2, kv2, *so_far)
    attended = attend(3, kv3, *so_far)

    summed = call(
        share_kernel,
        jax.ShapeDtypeStruct((chips, rows, width), BF16),
        "share",
        flops=4 * rows * width * chips * width,
    )(attended, other_core(attended), w_out, w_other)
    mesh_slots, mesh_back = call(sum_kernel, (state, low), "sum", bytes_accessed=1 << 20)(
        mesh_low, exchange(summed, "x")
    )

    returned = exchange(mesh_back.reshape(regions, cap, width), "region").reshape(slots, width)
    flat_nodes = slot_node[0].reshape(-1)
    node_hot = (jnp.arange(rows, dtype=jnp.int32)[:, None] == flat_nodes[None, :]).astype(F32)
    mesh_state = jnp.dot(
        node_hot, mesh_slots, precision=lax.Precision.HIGHEST, preferred_element_type=F32
    )
    gathered = jnp.dot(slot_hot.T, returned, preferred_element_type=F32)
    grid_out = (grid.astype(F32) + gathered).astype(BF16)
    return (mesh_state, grid_out)


def solution(mesh):
    regions, model = mesh.devices.shape
    split = Mesh(mesh.devices.reshape(regions, model // 2, 2), ("region", "x", "core"))
    model = ("x", "core")
    return jax.shard_map(
        on_device,
        mesh=split,
        in_specs=(
            P("region", model),
            P("region"),
            P("region"),
            P("region", None, None),
            P("region", None),
            P(),
            P(None, None, model),
            P(model, None),
        ),
        out_specs=(P("region", model), P("region", model)),
        check_vma=False,
    )
```

```python
import jax
import jax.numpy as jnp
from jax import lax
from jax.experimental import pallas as pl
from jax.experimental.pallas import tpu as pltpu
from jax.sharding import Mesh
from jax.sharding import PartitionSpec as P

HEAD_DIM = 64
OFFSETS = (-2, -1, 1, 2)
CHUNK = 128
BF16 = jnp.bfloat16
F32 = jnp.float32
VMEM = pl.BlockSpec(memory_space=pltpu.VMEM)
PARAMS = pltpu.CompilerParams(vmem_limit_bytes=32 * 1024 * 1024)


def exchange(array, axis):
    return lax.all_to_all(array, axis, split_axis=0, concat_axis=0, tiled=True)


def other_core(value):
    return lax.ppermute(value, "core", [(0, 1), (1, 0)])


def swapped(value, axis, first):
    count, cores = lax.axis_size(axis), lax.axis_size("core")
    pairs = []
    for place in range(count):
        for core in range(cores):
            ahead = ((place + core) % 2 == 0) == first
            partner = (place + (1 if ahead else -1)) % count
            pairs.append((place * cores + core, partner * cores + core))
    return lax.ppermute(value, (axis, "core"), pairs)


def after(value, *earlier):
    return lax.optimization_barrier((value, *earlier))[0]


def block_product(blocks, thirds, gain_ref, w_ref, scaled_ref, rows_ref, put):
    rows, width = blocks[0][0].shape
    for i, (_, index) in enumerate(blocks):
        source = pl.ds(pl.multiple_of(index * width, width), width)
        for at, third in enumerate(thirds):
            columns = slice(at * width, (at + 1) * width)
            rows_ref[i * width : (i + 1) * width, columns] = w_ref[third, source, :]

    def step(number, _):
        at = pl.ds(pl.multiple_of(number * CHUNK, CHUNK), CHUNK)
        total = jnp.zeros((CHUNK, width), F32)
        for i, (ref, index) in enumerate(blocks):
            value = ref[at, :].astype(F32)
            total = total + value * value
            gain = gain_ref[pl.ds(index, 1), :]
            scaled_ref[:, i * width : (i + 1) * width] = (value * gain).astype(BF16)
        put(at, total, jnp.dot(scaled_ref[...], rows_ref[...], preferred_element_type=F32))
        return 0

    lax.fori_loop(0, rows // CHUNK, step, 0)


def own_half_kernel(own_ref, gain_ref, w_ref, square_ref, product_ref, *scratch):
    core = lax.axis_index("core")

    def put(at, square, product):
        square_ref[at, :] = square
        product_ref[at, :] = product

    blocks = [(own_ref.at[chip], 2 * chip + core) for chip in range(own_ref.shape[0])]
    block_product(blocks, (0, 1, 2), gain_ref, w_ref, *scratch, put)


def finish(thirds, other_ref, gain_ref, w_ref, square0_ref, product0_ref, scratch, put):
    core = lax.axis_index("core")
    width = gain_ref.shape[1]
    features = gain_ref.shape[0] * width
    columns = slice(thirds[0] * width, (thirds[-1] + 1) * width)

    def add(at, square, product):
        mean = jnp.sum(square0_ref[at, :] + square, axis=-1, keepdims=True) / features
        factor = lax.rsqrt(mean + 1e-05)
        put(at, ((product0_ref[at, columns] + product) * factor).astype(BF16))

    blocks = [(other_ref.at[chip], 2 * chip + 1 - core) for chip in range(other_ref.shape[0])]
    block_product(blocks, thirds, gain_ref, w_ref, *scratch, add)


def kv_kernel(other_ref, gain_ref, w_ref, square0_ref, product0_ref, kv_ref, *scratch):
    rows, width = square0_ref.shape

    def put(at, both):
        kv_ref[at, :] = both[:, :width]
        kv_ref[pl.ds(pl.multiple_of(rows + at.start, CHUNK), CHUNK), :] = both[:, width:]

    finish((1, 2), other_ref, gain_ref, w_ref, square0_ref, product0_ref, scratch, put)


def q_kernel(other_ref, gain_ref, w_ref, square0_ref, product0_ref, q_ref, *scratch):
    def put(at, queries):
        q_ref[at, :] = queries

    finish((0,), other_ref, gain_ref, w_ref, square0_ref, product0_ref, scratch, put)


def attend_block(q_ref, kv_ref, seen, before, put):
    rows, width = q_ref.shape
    chunk = 256
    heads = width // HEAD_DIM
    lane = lax.broadcasted_iota(jnp.int32, (1, width), 1)
    keys = kv_ref[pl.ds(0, rows), :]
    values = kv_ref[pl.ds(rows, rows), :]
    summed = []
    for head in range(heads):
        mine = lane // HEAD_DIM == head
        ones = jnp.broadcast_to(jnp.where(mine, 1.0, 0.0), values.shape).astype(BF16)
        summed.append(jnp.concatenate([jnp.where(mine, values, 0).astype(BF16), ones], axis=1))
    for start in range(0, rows, chunk):
        at = pl.ds(start, chunk)
        queries = q_ref[at, :] * HEAD_DIM ** (-0.5)
        if before is not None:
            tops = before[0][at, :]
        new_tops = jnp.zeros((chunk, width), F32)
        gained = jnp.zeros((chunk, 2 * width), F32)
        for head in range(heads):
            mine = lane // HEAD_DIM == head
            scores = lax.dot_general(
                jnp.where(mine, queries, 0).astype(BF16),
                keys,
                (((1,), (1,)), ((), ())),
                preferred_element_type=F32,
            )
            if seen is not None:
                scores = jnp.where(seen, scores, -1e30)
            top = jnp.max(scores, axis=-1, keepdims=True)
            if before is not None:
                top = jnp.maximum(top, tops[:, head * HEAD_DIM : head * HEAD_DIM + 1])
            expd = jnp.exp(scores - top).astype(BF16)
            gained = gained + jnp.dot(expd, summed[head], preferred_element_type=F32)
            new_tops = jnp.where(mine, top, new_tops)
        mixed, total = gained[:, :width], gained[:, width:]
        if before is not None:
            shrink = jnp.exp(tops - new_tops)
            mixed = before[2][at, :] * shrink + mixed
            total = before[1][at, :] * shrink + total
        put(at, new_tops, total, mixed)


def is_seen(turn, mask_ref):
    odd = (lax.axis_index("region") + lax.axis_index("core")) & 1
    offset = (1, -1, -2, 2)[turn]
    wanted = jnp.where(odd == 0, OFFSETS.index(offset), OFFSETS.index(-offset))
    mask = mask_ref[...]
    lane = lax.broadcasted_iota(jnp.int32, mask.shape, 1)
    return jnp.sum(jnp.where(lane == wanted, mask, 0), axis=-1, keepdims=True) > 0


def own_kernel(q_ref, kv_ref, *states):
    def put(at, *values):
        for ref, value in zip(states, values):
            ref[at, :] = value

    attend_block(q_ref, kv_ref, None, None, put)


def peer_kernel(turn, mask_ref, q_ref, kv_ref, *states):
    def put(at, *values):
        for ref, value in zip(states[3:], values):
            ref[at, :] = value

    attend_block(q_ref, kv_ref, is_seen(turn, mask_ref), states[:3], put)


def last_kernel(turn, mask_ref, q_ref, kv_ref, *refs):
    def put(at, top, total, mixed):
        refs[3][at, :] = (mixed / total).astype(BF16)

    attend_block(q_ref, kv_ref, is_seen(turn, mask_ref), refs[:3], put)


def share_kernel(own_ref, other_ref, w_own_ref, w_other_ref, out_ref):
    blocks, _, width = out_ref.shape
    core = lax.axis_index("core")
    both = jnp.concatenate([own_ref[...], other_ref[...]], axis=1)
    for block in range(blocks):
        at = pl.ds(pl.multiple_of((2 * block + core) * width, width), width)
        weight = jnp.concatenate([w_own_ref[:, at], w_other_ref[:, at]], axis=0)
        out_ref[block] = jnp.dot(both, weight, preferred_element_type=F32).astype(BF16)


def sum_kernel(base_ref, parts_ref, state_ref, back_ref):
    total = base_ref[...].astype(F32)
    for block in range(parts_ref.shape[0]):
        total = total + parts_ref[block].astype(F32)
    state_ref[...] = total
    back_ref[...] = total.astype(BF16)


def down(row):
    return jnp.broadcast_to(row, (row.shape[1], row.shape[1])).T


def decode_kernel(slot_ref, returned_ref, grid_ref, out_ref):
    step = pl.program_id(0)
    points, lanes = grid_ref.shape
    slots = returned_ref.shape[0]
    pieces = points // lanes
    for i in range(pieces):
        slot = down(slot_ref[pl.ds(step * pieces + i, 1), :])
        number = lax.broadcasted_iota(jnp.int32, (lanes, slots), 1)
        hot = jnp.where(number == jnp.concatenate([slot] * (slots // lanes), axis=1), 1.0, 0.0)
        rows = slice(i * lanes, (i + 1) * lanes)
        back = jnp.dot(hot.astype(BF16), returned_ref[...], preferred_element_type=F32)
        out_ref[rows, :] = (grid_ref[rows, :].astype(F32) + back).astype(BF16)


def call(kernel, outs, name, scratch=(), flops=0, bytes_accessed=0, transcendentals=0):
    def run(*args):
        return pl.pallas_call(
            kernel,
            out_shape=outs,
            in_specs=[VMEM] * len(args),
            out_specs=jax.tree.map(lambda _: VMEM, outs),
            scratch_shapes=list(scratch),
            compiler_params=PARAMS,
            name=name,
            cost_estimate=pl.CostEstimate(
                flops=flops, bytes_accessed=bytes_accessed, transcendentals=transcendentals
            ),
        )(*args)

    return run


def on_device(grid, g2m_weight, g2m_slot, slot_node, peer_mask, norm_gain, w_qkv, w_out):
    regions = lax.axis_size("region")
    chips = lax.axis_size("x")
    parts = chips * lax.axis_size("core")
    cap = slot_node.shape[2]
    slots = regions * cap
    rows = slots
    width = grid.shape[1]
    low = jax.ShapeDtypeStruct((rows, width), BF16)
    state = jax.ShapeDtypeStruct((rows, width), F32)

    points = grid.shape[0]
    by_lane = pl.BlockSpec((points // width, width), lambda i: (0, 0))
    by_slot = pl.BlockSpec((slots, width), lambda i: (0, 0))
    by_step = pl.BlockSpec((points // 4, width), lambda i: (i, 0))
    slot_rows = g2m_slot.reshape(-1, width)
    scaled = (g2m_weight[:, None] * grid.astype(F32)).astype(BF16)
    slot_hot = (g2m_slot[None, :] == jnp.arange(slots, dtype=jnp.int32)[:, None]).astype(BF16)
    partial_value = jnp.dot(slot_hot, scaled, preferred_element_type=F32).astype(BF16)
    w_other = other_core(w_out)
    mesh_low = exchange(partial_value.reshape(regions, cap, width), "region").reshape(rows, width)

    mesh_low = after(mesh_low, w_other)
    own = exchange(jnp.broadcast_to(mesh_low, (chips, rows, width)), "x")
    other = other_core(own)
    gain = norm_gain.reshape(parts, width)

    def product(kernel, outs, name, thirds, *args):
        depth = chips * width
        return call(
            kernel,
            outs,
            name,
            scratch=[pltpu.VMEM((CHUNK, depth), BF16), pltpu.VMEM((depth, thirds * width), BF16)],
            flops=2 * thirds * rows * depth * width,
            bytes_accessed=2 << 20,
        )(*args)

    sums = (state, jax.ShapeDtypeStruct((rows, 3 * width), F32))
    kvs = jax.ShapeDtypeStruct((2 * rows, width), BF16)
    so_far = product(own_half_kernel, sums, "own_half", 3, own, gain, w_qkv)
    kv = product(kv_kernel, kvs, "kv", 2, other, gain, w_qkv, *so_far)
    queries = product(q_kernel, low, "q", 1, other, gain, w_qkv, *so_far)

    cost = dict(flops=8 * rows * rows * width, transcendentals=2 * rows * rows)

    def attend(turn, *args):
        outs, kernel = (low, last_kernel) if turn == 3 else ((state,) * 3, peer_kernel)
        return call(lambda *refs: kernel(turn, *refs), outs, f"peer{turn}", **cost)(
            peer_mask, queries, *args
        )

    kv0 = swapped(kv, "region", True)
    kv1 = swapped(kv, "region", False)
    so_far = call(own_kernel, (state,) * 3, "own", **cost)(queries, kv)
    kv2 = swapped(after(kv0, so_far[0]), "region", False)
    kv3 = swapped(kv1, "region", True)
    so_far = attend(0, kv0, *so_far)
    so_far = attend(1, kv1, *so_far)
    so_far = attend(2, kv2, *so_far)
    attended = attend(3, kv3, *so_far)

    summed = call(
        share_kernel,
        jax.ShapeDtypeStruct((chips, rows, width), BF16),
        "share",
        flops=4 * rows * width * chips * width,
    )(attended, other_core(attended), w_out, w_other)
    mesh_slots, mesh_back = call(sum_kernel, (state, low), "sum", bytes_accessed=1 << 20)(
        mesh_low, exchange(summed, "x")
    )

    returned = exchange(mesh_back.reshape(regions, cap, width), "region").reshape(slots, width)
    flat_nodes = slot_node[0].reshape(-1)
    node_hot = (jnp.arange(rows, dtype=jnp.int32)[:, None] == flat_nodes[None, :]).astype(F32)
    mesh_state = jnp.dot(
        node_hot, mesh_slots, precision=lax.Precision.HIGHEST, preferred_element_type=F32
    )
    grid_out = pl.pallas_call(
        decode_kernel,
        grid=(4,),
        out_shape=jax.ShapeDtypeStruct(grid.shape, BF16),
        in_specs=[by_lane, by_slot, by_step],
        out_specs=by_step,
        compiler_params=PARAMS,
        name="decode",
    )(slot_rows, returned, grid)
    return (mesh_state, grid_out)


def solution(mesh):
    regions, model = mesh.devices.shape
    split = Mesh(mesh.devices.reshape(regions, model // 2, 2), ("region", "x", "core"))
    model = ("x", "core")
    return jax.shard_map(
        on_device,
        mesh=split,
        in_specs=(
            P("region", model),
            P("region"),
            P("region"),
            P("region", None, None),
            P("region", None),
            P(),
            P(None, None, model),
            P(model, None),
        ),
        out_specs=(P("region", model), P("region", model)),
        check_vma=False,
    )
```

```python
import jax
import jax.numpy as jnp
from jax import lax
from jax.experimental import pallas as pl
from jax.experimental.pallas import tpu as pltpu
from jax.sharding import Mesh
from jax.sharding import PartitionSpec as P

HEAD_DIM = 64
OFFSETS = (-2, -1, 1, 2)
CHUNK = 128
BF16 = jnp.bfloat16
F32 = jnp.float32
VMEM = pl.BlockSpec(memory_space=pltpu.VMEM)
PARAMS = pltpu.CompilerParams(vmem_limit_bytes=32 * 1024 * 1024)


def exchange(array, axis):
    return lax.all_to_all(array, axis, split_axis=0, concat_axis=0, tiled=True)


def other_core(value):
    return lax.ppermute(value, "core", [(0, 1), (1, 0)])


def swapped(value, axis, first):
    count, cores = lax.axis_size(axis), lax.axis_size("core")
    pairs = []
    for place in range(count):
        for core in range(cores):
            ahead = ((place + core) % 2 == 0) == first
            partner = (place + (1 if ahead else -1)) % count
            pairs.append((place * cores + core, partner * cores + core))
    return lax.ppermute(value, (axis, "core"), pairs)


def after(value, *earlier):
    return lax.optimization_barrier((value, *earlier))[0]


def block_product(blocks, thirds, gain_ref, w_ref, scaled_ref, rows_ref, put):
    rows, width = blocks[0][0].shape
    for i, (_, index) in enumerate(blocks):
        source = pl.ds(pl.multiple_of(index * width, width), width)
        for at, third in enumerate(thirds):
            columns = slice(at * width, (at + 1) * width)
            rows_ref[i * width : (i + 1) * width, columns] = w_ref[third, source, :]

    def step(number, _):
        at = pl.ds(pl.multiple_of(number * CHUNK, CHUNK), CHUNK)
        total = jnp.zeros((CHUNK, width), F32)
        for i, (ref, index) in enumerate(blocks):
            value = ref[at, :].astype(F32)
            total = total + value * value
            gain = gain_ref[pl.ds(index, 1), :]
            scaled_ref[:, i * width : (i + 1) * width] = (value * gain).astype(BF16)
        put(at, total, jnp.dot(scaled_ref[...], rows_ref[...], preferred_element_type=F32))
        return 0

    lax.fori_loop(0, rows // CHUNK, step, 0)


def own_half_kernel(own_ref, gain_ref, w_ref, square_ref, product_ref, *scratch):
    core = lax.axis_index("core")

    def put(at, square, product):
        square_ref[at, :] = square
        product_ref[at, :] = product

    blocks = [(own_ref.at[chip], 2 * chip + core) for chip in range(own_ref.shape[0])]
    block_product(blocks, (0, 1, 2), gain_ref, w_ref, *scratch, put)


def finish(thirds, other_ref, gain_ref, w_ref, square0_ref, product0_ref, scratch, put):
    core = lax.axis_index("core")
    width = gain_ref.shape[1]
    features = gain_ref.shape[0] * width
    columns = slice(thirds[0] * width, (thirds[-1] + 1) * width)

    def add(at, square, product):
        mean = jnp.sum(square0_ref[at, :] + square, axis=-1, keepdims=True) / features
        factor = lax.rsqrt(mean + 1e-05)
        put(at, ((product0_ref[at, columns] + product) * factor).astype(BF16))

    blocks = [(other_ref.at[chip], 2 * chip + 1 - core) for chip in range(other_ref.shape[0])]
    block_product(blocks, thirds, gain_ref, w_ref, *scratch, add)


def kv_kernel(other_ref, gain_ref, w_ref, square0_ref, product0_ref, kv_ref, *scratch):
    rows, width = square0_ref.shape

    def put(at, both):
        kv_ref[at, :] = both[:, :width]
        kv_ref[pl.ds(pl.multiple_of(rows + at.start, CHUNK), CHUNK), :] = both[:, width:]

    finish((1, 2), other_ref, gain_ref, w_ref, square0_ref, product0_ref, scratch, put)


def q_kernel(other_ref, gain_ref, w_ref, square0_ref, product0_ref, q_ref, *scratch):
    def put(at, queries):
        q_ref[at, :] = queries

    finish((0,), other_ref, gain_ref, w_ref, square0_ref, product0_ref, scratch, put)


def attend_block(q_ref, kv_ref, seen, before, put):
    rows, width = q_ref.shape
    chunk = 256
    heads = width // HEAD_DIM
    lane = lax.broadcasted_iota(jnp.int32, (1, width), 1)
    keys = kv_ref[pl.ds(0, rows), :]
    values = kv_ref[pl.ds(rows, rows), :]
    summed = []
    for head in range(heads):
        mine = lane // HEAD_DIM == head
        ones = jnp.broadcast_to(jnp.where(mine, 1.0, 0.0), values.shape).astype(BF16)
        summed.append(jnp.concatenate([jnp.where(mine, values, 0).astype(BF16), ones], axis=1))
    for start in range(0, rows, chunk):
        at = pl.ds(start, chunk)
        queries = q_ref[at, :] * HEAD_DIM ** (-0.5)
        if before is not None:
            tops = before[0][at, :]
        new_tops = jnp.zeros((chunk, width), F32)
        gained = jnp.zeros((chunk, 2 * width), F32)
        for head in range(heads):
            mine = lane // HEAD_DIM == head
            scores = lax.dot_general(
                jnp.where(mine, queries, 0).astype(BF16),
                keys,
                (((1,), (1,)), ((), ())),
                preferred_element_type=F32,
            )
            if seen is not None:
                scores = jnp.where(seen, scores, -1e30)
            top = jnp.max(scores, axis=-1, keepdims=True)
            if before is not None:
                top = jnp.maximum(top, tops[:, head * HEAD_DIM : head * HEAD_DIM + 1])
            expd = jnp.exp(scores - top).astype(BF16)
            gained = gained + jnp.dot(expd, summed[head], preferred_element_type=F32)
            new_tops = jnp.where(mine, top, new_tops)
        mixed, total = gained[:, :width], gained[:, width:]
        if before is not None:
            shrink = jnp.exp(tops - new_tops)
            mixed = before[2][at, :] * shrink + mixed
            total = before[1][at, :] * shrink + total
        put(at, new_tops, total, mixed)


def is_seen(turn, mask_ref):
    odd = (lax.axis_index("region") + lax.axis_index("core")) & 1
    offset = (1, -1, -2, 2)[turn]
    wanted = jnp.where(odd == 0, OFFSETS.index(offset), OFFSETS.index(-offset))
    mask = mask_ref[...]
    lane = lax.broadcasted_iota(jnp.int32, mask.shape, 1)
    return jnp.sum(jnp.where(lane == wanted, mask, 0), axis=-1, keepdims=True) > 0


def own_kernel(q_ref, kv_ref, *states):
    def put(at, *values):
        for ref, value in zip(states, values):
            ref[at, :] = value

    attend_block(q_ref, kv_ref, None, None, put)


def peer_kernel(turn, mask_ref, q_ref, kv_ref, *states):
    def put(at, *values):
        for ref, value in zip(states[3:], values):
            ref[at, :] = value

    attend_block(q_ref, kv_ref, is_seen(turn, mask_ref), states[:3], put)


def last_kernel(turn, mask_ref, q_ref, kv_ref, top_ref, total_ref, mixed_ref, w_ref, out_ref):
    rows, width = q_ref.shape

    def put(at, top, total, mixed):
        out_ref[at, :] = (mixed / total).astype(BF16)

    attend_block(q_ref, kv_ref, is_seen(turn, mask_ref), (top_ref, total_ref, mixed_ref), put)
    part = 1 - lax.axis_index("core")
    for block in range(w_ref.shape[1] // (2 * width)):
        at = pl.ds(pl.multiple_of((2 * block + part) * width, width), width)
        out_ref[rows + block * width : rows + (block + 1) * width, :] = w_ref[:, at]


def share_kernel(chip_ref, w_ref, out_ref):
    blocks, rows, width = out_ref.shape
    core = lax.axis_index("core")
    both = jnp.concatenate([chip_ref[core, :rows, :], chip_ref[1 - core, :rows, :]], axis=1)
    for block in range(blocks):
        at = pl.ds(pl.multiple_of((2 * block + core) * width, width), width)
        w_other = chip_ref[1 - core, rows + block * width : rows + (block + 1) * width, :]
        weight = jnp.concatenate([w_ref[:, at], w_other], axis=0)
        out_ref[block] = jnp.dot(both, weight, preferred_element_type=F32).astype(BF16)


def sum_kernel(base_ref, parts_ref, state_ref, back_ref):
    total = base_ref[...].astype(F32)
    for block in range(parts_ref.shape[0]):
        total = total + parts_ref[block].astype(F32)
    state_ref[...] = total
    back_ref[...] = total.astype(BF16)


def call(kernel, outs, name, scratch=(), flops=0, bytes_accessed=0, transcendentals=0):
    def run(*args):
        return pl.pallas_call(
            kernel,
            out_shape=outs,
            in_specs=[VMEM] * len(args),
            out_specs=jax.tree.map(lambda _: VMEM, outs),
            scratch_shapes=list(scratch),
            compiler_params=PARAMS,
            name=name,
            cost_estimate=pl.CostEstimate(
                flops=flops, bytes_accessed=bytes_accessed, transcendentals=transcendentals
            ),
        )(*args)

    return run


def on_device(grid, g2m_weight, g2m_slot, slot_node, peer_mask, norm_gain, w_qkv, w_out):
    regions = lax.axis_size("region")
    chips = lax.axis_size("x")
    parts = chips * lax.axis_size("core")
    cap = slot_node.shape[2]
    slots = regions * cap
    rows = slots
    width = grid.shape[1]
    low = jax.ShapeDtypeStruct((rows, width), BF16)
    state = jax.ShapeDtypeStruct((rows, width), F32)

    scaled = (g2m_weight[:, None] * grid.astype(F32)).astype(BF16)
    slot_hot = (g2m_slot[None, :] == jnp.arange(slots, dtype=jnp.int32)[:, None]).astype(BF16)
    partial_value = jnp.dot(slot_hot, scaled, preferred_element_type=F32).astype(BF16)
    mesh_low = exchange(partial_value.reshape(regions, cap, width), "region").reshape(rows, width)

    own = exchange(jnp.broadcast_to(mesh_low, (chips, rows, width)), "x")
    other = other_core(own)
    gain = norm_gain.reshape(parts, width)

    def product(kernel, outs, name, thirds, *args):
        depth = chips * width
        return call(
            kernel,
            outs,
            name,
            scratch=[pltpu.VMEM((CHUNK, depth), BF16), pltpu.VMEM((depth, thirds * width), BF16)],
            flops=2 * thirds * rows * depth * width,
            bytes_accessed=2 << 20,
        )(*args)

    sums = (state, jax.ShapeDtypeStruct((rows, 3 * width), F32))
    kvs = jax.ShapeDtypeStruct((2 * rows, width), BF16)
    so_far = product(own_half_kernel, sums, "own_half", 3, own, gain, w_qkv)
    kv = product(kv_kernel, kvs, "kv", 2, other, gain, w_qkv, *so_far)
    queries = product(q_kernel, low, "q", 1, other, gain, w_qkv, *so_far)

    cost = dict(flops=8 * rows * rows * width, transcendentals=2 * rows * rows)

    def attend(turn, *args):
        lasts = jax.ShapeDtypeStruct((rows + chips * width, width), BF16)
        outs, kernel = (lasts, last_kernel) if turn == 3 else ((state,) * 3, peer_kernel)
        return call(lambda *refs: kernel(turn, *refs), outs, f"peer{turn}", **cost)(
            peer_mask, queries, *args
        )

    kv0 = swapped(kv, "region", True)
    kv1 = swapped(kv, "region", False)
    so_far = call(own_kernel, (state,) * 3, "own", **cost)(queries, kv)
    kv2 = swapped(after(kv0, so_far[0]), "region", False)
    kv3 = swapped(kv1, "region", True)
    so_far = attend(0, kv0, *so_far)
    so_far = attend(1, kv1, *so_far)
    so_far = attend(2, kv2, *so_far)
    attended = attend(3, kv3, *so_far, w_out)

    summed = call(
        share_kernel,
        jax.ShapeDtypeStruct((chips, rows, width), BF16),
        "share",
        flops=4 * rows * width * chips * width,
    )(lax.all_gather(attended, "core"), w_out)
    mesh_slots, mesh_back = call(sum_kernel, (state, low), "sum", bytes_accessed=1 << 20)(
        mesh_low, exchange(summed, "x")
    )

    returned = exchange(mesh_back.reshape(regions, cap, width), "region").reshape(slots, width)
    flat_nodes = slot_node[0].reshape(-1)
    node_hot = (jnp.arange(rows, dtype=jnp.int32)[:, None] == flat_nodes[None, :]).astype(F32)
    mesh_state = jnp.dot(
        node_hot, mesh_slots, precision=lax.Precision.HIGHEST, preferred_element_type=F32
    )
    gathered = jnp.dot(slot_hot.T, returned, preferred_element_type=F32)
    grid_out = (grid.astype(F32) + gathered).astype(BF16)
    return (mesh_state, grid_out)


def solution(mesh):
    regions, model = mesh.devices.shape
    split = Mesh(mesh.devices.reshape(regions, model // 2, 2), ("region", "x", "core"))
    model = ("x", "core")
    return jax.shard_map(
        on_device,
        mesh=split,
        in_specs=(
            P("region", model),
            P("region"),
            P("region"),
            P("region", None, None),
            P("region", None),
            P(),
            P(None, None, model),
            P(model, None),
        ),
        out_specs=(P("region", model), P("region", model)),
        check_vma=False,
    )
```

```python
import jax
import jax.numpy as jnp
from jax import lax
from jax.experimental import pallas as pl
from jax.experimental.pallas import tpu as pltpu
from jax.sharding import Mesh
from jax.sharding import PartitionSpec as P

HEAD_DIM = 64
OFFSETS = (-2, -1, 1, 2)
CHUNK = 256
BF16 = jnp.bfloat16
F32 = jnp.float32
VMEM = pl.BlockSpec(memory_space=pltpu.VMEM)
PARAMS = pltpu.CompilerParams(vmem_limit_bytes=32 * 1024 * 1024)


def exchange(array, axis):
    return lax.all_to_all(array, axis, split_axis=0, concat_axis=0, tiled=True)


def other_core(value):
    return lax.ppermute(value, "core", [(0, 1), (1, 0)])


def swapped(value, axis, first):
    count, cores = lax.axis_size(axis), lax.axis_size("core")
    pairs = []
    for place in range(count):
        for core in range(cores):
            ahead = ((place + core) % 2 == 0) == first
            partner = (place + (1 if ahead else -1)) % count
            pairs.append((place * cores + core, partner * cores + core))
    return lax.ppermute(value, (axis, "core"), pairs)


def after(value, *earlier):
    return lax.optimization_barrier((value, *earlier))[0]


def block_product(blocks, thirds, gain_ref, w_ref, scaled_ref, rows_ref, put):
    rows, width = blocks[0][0].shape
    for i, (_, index) in enumerate(blocks):
        source = pl.ds(pl.multiple_of(index * width, width), width)
        for at, third in enumerate(thirds):
            columns = slice(at * width, (at + 1) * width)
            rows_ref[i * width : (i + 1) * width, columns] = w_ref[third, source, :]

    def step(number, _):
        at = pl.ds(pl.multiple_of(number * CHUNK, CHUNK), CHUNK)
        total = jnp.zeros((CHUNK, width), F32)
        for i, (ref, index) in enumerate(blocks):
            value = ref[at, :].astype(F32)
            total = total + value * value
            gain = gain_ref[pl.ds(index, 1), :]
            scaled_ref[:, i * width : (i + 1) * width] = (value * gain).astype(BF16)
        put(at, total, jnp.dot(scaled_ref[...], rows_ref[...], preferred_element_type=F32))
        return 0

    lax.fori_loop(0, rows // CHUNK, step, 0)


def own_half_kernel(own_ref, gain_ref, w_ref, square_ref, product_ref, *scratch):
    core = lax.axis_index("core")

    def put(at, square, product):
        square_ref[at, :] = square
        product_ref[at, :] = product

    blocks = [(own_ref.at[chip], 2 * chip + core) for chip in range(own_ref.shape[0])]
    block_product(blocks, (0, 1, 2), gain_ref, w_ref, *scratch, put)


def finish(thirds, other_ref, gain_ref, w_ref, square0_ref, product0_ref, scratch, put):
    core = lax.axis_index("core")
    width = gain_ref.shape[1]
    features = gain_ref.shape[0] * width
    columns = slice(thirds[0] * width, (thirds[-1] + 1) * width)

    def add(at, square, product):
        mean = jnp.sum(square0_ref[at, :] + square, axis=-1, keepdims=True) / features
        factor = lax.rsqrt(mean + 1e-05)
        put(at, ((product0_ref[at, columns] + product) * factor).astype(BF16))

    blocks = [(other_ref.at[chip], 2 * chip + 1 - core) for chip in range(other_ref.shape[0])]
    block_product(blocks, thirds, gain_ref, w_ref, *scratch, add)


def kv_kernel(other_ref, gain_ref, w_ref, square0_ref, product0_ref, kv_ref, *scratch):
    rows, width = square0_ref.shape

    def put(at, both):
        kv_ref[at, :] = both[:, :width]
        kv_ref[pl.ds(pl.multiple_of(rows + at.start, CHUNK), CHUNK), :] = both[:, width:]

    finish((1, 2), other_ref, gain_ref, w_ref, square0_ref, product0_ref, scratch, put)


def q_kernel(other_ref, gain_ref, w_ref, square0_ref, product0_ref, q_ref, *scratch):
    def put(at, queries):
        q_ref[at, :] = queries

    finish((0,), other_ref, gain_ref, w_ref, square0_ref, product0_ref, scratch, put)


def attend_block(q_ref, kv_ref, seen, before, put):
    rows, width = q_ref.shape
    chunk = 256
    heads = width // HEAD_DIM
    lane = lax.broadcasted_iota(jnp.int32, (1, width), 1)
    keys = kv_ref[pl.ds(0, rows), :]
    values = kv_ref[pl.ds(rows, rows), :]
    summed = []
    for head in range(heads):
        mine = lane // HEAD_DIM == head
        ones = jnp.broadcast_to(jnp.where(mine, 1.0, 0.0), values.shape).astype(BF16)
        summed.append(jnp.concatenate([jnp.where(mine, values, 0).astype(BF16), ones], axis=1))
    for start in range(0, rows, chunk):
        at = pl.ds(start, chunk)
        queries = q_ref[at, :] * HEAD_DIM ** (-0.5)
        if before is not None:
            tops = before[0][at, :]
        new_tops = jnp.zeros((chunk, width), F32)
        gained = jnp.zeros((chunk, 2 * width), F32)
        for head in range(heads):
            mine = lane // HEAD_DIM == head
            scores = lax.dot_general(
                jnp.where(mine, queries, 0).astype(BF16),
                keys,
                (((1,), (1,)), ((), ())),
                preferred_element_type=F32,
            )
            if seen is not None:
                scores = jnp.where(seen, scores, -1e30)
            top = jnp.max(scores, axis=-1, keepdims=True)
            if before is not None:
                top = jnp.maximum(top, tops[:, head * HEAD_DIM : head * HEAD_DIM + 1])
            expd = jnp.exp(scores - top).astype(BF16)
            gained = gained + jnp.dot(expd, summed[head], preferred_element_type=F32)
            new_tops = jnp.where(mine, top, new_tops)
        mixed, total = gained[:, :width], gained[:, width:]
        if before is not None:
            shrink = jnp.exp(tops - new_tops)
            mixed = before[2][at, :] * shrink + mixed
            total = before[1][at, :] * shrink + total
        put(at, new_tops, total, mixed)


def is_seen(turn, mask_ref):
    odd = (lax.axis_index("region") + lax.axis_index("core")) & 1
    offset = (1, -1, -2, 2)[turn]
    wanted = jnp.where(odd == 0, OFFSETS.index(offset), OFFSETS.index(-offset))
    mask = mask_ref[...]
    lane = lax.broadcasted_iota(jnp.int32, mask.shape, 1)
    return jnp.sum(jnp.where(lane == wanted, mask, 0), axis=-1, keepdims=True) > 0


def own_kernel(q_ref, kv_ref, *states):
    def put(at, *values):
        for ref, value in zip(states, values):
            ref[at, :] = value

    attend_block(q_ref, kv_ref, None, None, put)


def peer_kernel(turn, mask_ref, q_ref, kv_ref, *states):
    def put(at, *values):
        for ref, value in zip(states[3:], values):
            ref[at, :] = value

    attend_block(q_ref, kv_ref, is_seen(turn, mask_ref), states[:3], put)


def last_kernel(turn, mask_ref, q_ref, kv_ref, top_ref, total_ref, mixed_ref, w_ref, out_ref):
    rows, width = q_ref.shape

    def put(at, top, total, mixed):
        out_ref[at, :] = (mixed / total).astype(BF16)

    attend_block(q_ref, kv_ref, is_seen(turn, mask_ref), (top_ref, total_ref, mixed_ref), put)
    part = 1 - lax.axis_index("core")
    for block in range(w_ref.shape[1] // (2 * width)):
        at = pl.ds(pl.multiple_of((2 * block + part) * width, width), width)
        out_ref[rows + block * width : rows + (block + 1) * width, :] = w_ref[:, at]


def share_kernel(chip_ref, w_ref, out_ref):
    blocks, rows, width = out_ref.shape
    core = lax.axis_index("core")
    both = jnp.concatenate([chip_ref[core, :rows, :], chip_ref[1 - core, :rows, :]], axis=1)
    for block in range(blocks):
        at = pl.ds(pl.multiple_of((2 * block + core) * width, width), width)
        w_other = chip_ref[1 - core, rows + block * width : rows + (block + 1) * width, :]
        weight = jnp.concatenate([w_ref[:, at], w_other], axis=0)
        out_ref[block] = jnp.dot(both, weight, preferred_element_type=F32).astype(BF16)


def sum_kernel(base_ref, parts_ref, state_ref, back_ref):
    total = base_ref[...].astype(F32)
    for block in range(parts_ref.shape[0]):
        total = total + parts_ref[block].astype(F32)
    state_ref[...] = total
    back_ref[...] = total.astype(BF16)


def hot_kernel(slot_ref, hot_ref):
    lanes, slots = slot_ref.shape[1], hot_ref.shape[1]
    number = lax.broadcasted_iota(jnp.int32, (lanes, slots), 1)
    for i in range(slot_ref.shape[0]):
        down = jnp.broadcast_to(slot_ref[i : i + 1, :], (lanes, lanes)).T
        wanted = jnp.concatenate([down] * (slots // lanes), axis=1)
        hot_ref[i * lanes : (i + 1) * lanes, :] = jnp.where(number == wanted, 1.0, 0.0).astype(BF16)


def decode_kernel(hot_ref, returned_ref, grid_ref, out_ref):
    back = jnp.dot(hot_ref[...], returned_ref[...], preferred_element_type=F32)
    out_ref[...] = (grid_ref[...].astype(F32) + back).astype(BF16)


def call(kernel, outs, name, scratch=(), flops=0, bytes_accessed=0, transcendentals=0):
    def run(*args):
        return pl.pallas_call(
            kernel,
            out_shape=outs,
            in_specs=[VMEM] * len(args),
            out_specs=jax.tree.map(lambda _: VMEM, outs),
            scratch_shapes=list(scratch),
            compiler_params=PARAMS,
            name=name,
            cost_estimate=pl.CostEstimate(
                flops=flops, bytes_accessed=bytes_accessed, transcendentals=transcendentals
            ),
        )(*args)

    return run


def on_device(grid, g2m_weight, g2m_slot, slot_node, peer_mask, norm_gain, w_qkv, w_out):
    regions = lax.axis_size("region")
    chips = lax.axis_size("x")
    parts = chips * lax.axis_size("core")
    cap = slot_node.shape[2]
    slots = regions * cap
    rows = slots
    width = grid.shape[1]
    low = jax.ShapeDtypeStruct((rows, width), BF16)
    state = jax.ShapeDtypeStruct((rows, width), F32)

    scaled = (g2m_weight[:, None] * grid.astype(F32)).astype(BF16)
    slot_hot = (g2m_slot[None, :] == jnp.arange(slots, dtype=jnp.int32)[:, None]).astype(BF16)
    partial_value = jnp.dot(slot_hot, scaled, preferred_element_type=F32).astype(BF16)
    mesh_low = exchange(partial_value.reshape(regions, cap, width), "region").reshape(rows, width)

    own = exchange(jnp.broadcast_to(mesh_low, (chips, rows, width)), "x")
    other = other_core(own)
    gain = norm_gain.reshape(parts, width)

    def product(kernel, outs, name, thirds, *args):
        depth = chips * width
        return call(
            kernel,
            outs,
            name,
            scratch=[pltpu.VMEM((CHUNK, depth), BF16), pltpu.VMEM((depth, thirds * width), BF16)],
            flops=2 * thirds * rows * depth * width,
            bytes_accessed=2 << 20,
        )(*args)

    sums = (state, jax.ShapeDtypeStruct((rows, 3 * width), F32))
    kvs = jax.ShapeDtypeStruct((2 * rows, width), BF16)
    so_far = product(own_half_kernel, sums, "own_half", 3, own, gain, w_qkv)
    kv = product(kv_kernel, kvs, "kv", 2, other, gain, w_qkv, *so_far)
    queries = product(q_kernel, low, "q", 1, other, gain, w_qkv, *so_far)

    cost = dict(flops=8 * rows * rows * width, transcendentals=2 * rows * rows)

    def attend(turn, *args):
        lasts = jax.ShapeDtypeStruct((rows + chips * width, width), BF16)
        outs, kernel = (lasts, last_kernel) if turn == 3 else ((state,) * 3, peer_kernel)
        return call(lambda *refs: kernel(turn, *refs), outs, f"peer{turn}", **cost)(
            peer_mask, queries, *args
        )

    kv0 = swapped(kv, "region", True)
    kv1 = swapped(kv, "region", False)
    so_far = call(own_kernel, (state,) * 3, "own", **cost)(queries, kv)
    kv2 = swapped(after(kv0, so_far[0]), "region", False)
    kv3 = swapped(kv1, "region", True)
    so_far = attend(0, kv0, *so_far)
    so_far = attend(1, kv1, *so_far)
    so_far = attend(2, kv2, *so_far)
    attended = attend(3, kv3, *so_far, w_out)

    summed = call(
        share_kernel,
        jax.ShapeDtypeStruct((chips, rows, width), BF16),
        "share",
        flops=4 * rows * width * chips * width,
    )(lax.all_gather(attended, "core"), w_out)
    mesh_slots, mesh_back = call(sum_kernel, (state, low), "sum", bytes_accessed=1 << 20)(
        mesh_low, exchange(summed, "x")
    )

    returned = exchange(mesh_back.reshape(regions, cap, width), "region").reshape(slots, width)
    flat_nodes = slot_node[0].reshape(-1)
    node_hot = (jnp.arange(rows, dtype=jnp.int32)[:, None] == flat_nodes[None, :]).astype(F32)
    mesh_state = jnp.dot(
        node_hot, mesh_slots, precision=lax.Precision.HIGHEST, preferred_element_type=F32
    )
    hots = jax.ShapeDtypeStruct((grid.shape[0], slots), BF16)
    slot_rows = after(g2m_slot.reshape(-1, width), mesh_back)
    hot = call(hot_kernel, hots, "hot", bytes_accessed=1 << 21)(slot_rows)
    outs = jax.ShapeDtypeStruct(grid.shape, BF16)
    grid_out = call(decode_kernel, outs, "decode")(hot, returned, grid)
    return (mesh_state, grid_out)


def solution(mesh):
    regions, model = mesh.devices.shape
    split = Mesh(mesh.devices.reshape(regions, model // 2, 2), ("region", "x", "core"))
    model = ("x", "core")
    return jax.shard_map(
        on_device,
        mesh=split,
        in_specs=(
            P("region", model),
            P("region"),
            P("region"),
            P("region", None, None),
            P("region", None),
            P(),
            P(None, None, model),
            P(model, None),
        ),
        out_specs=(P("region", model), P("region", model)),
        check_vma=False,
    )
```

```python
import jax
import jax.numpy as jnp
from jax import lax
from jax.experimental import pallas as pl
from jax.experimental.pallas import tpu as pltpu
from jax.sharding import Mesh
from jax.sharding import PartitionSpec as P

HEAD_DIM = 64
OFFSETS = (-2, -1, 1, 2)
CHUNK = 256
BF16 = jnp.bfloat16
F32 = jnp.float32
VMEM = pl.BlockSpec(memory_space=pltpu.VMEM)
PARAMS = pltpu.CompilerParams(vmem_limit_bytes=32 * 1024 * 1024)


def exchange(array, axis):
    return lax.all_to_all(array, axis, split_axis=0, concat_axis=0, tiled=True)


def other_core(value):
    return lax.ppermute(value, "core", [(0, 1), (1, 0)])


def swapped(value, axis, first):
    count, cores = lax.axis_size(axis), lax.axis_size("core")
    pairs = []
    for place in range(count):
        for core in range(cores):
            ahead = ((place + core) % 2 == 0) == first
            partner = (place + (1 if ahead else -1)) % count
            pairs.append((place * cores + core, partner * cores + core))
    return lax.ppermute(value, (axis, "core"), pairs)


def after(value, *earlier):
    return lax.optimization_barrier((value, *earlier))[0]


def block_product(blocks, thirds, gain_ref, w_ref, scaled_ref, rows_ref, put):
    rows, width = blocks[0][0].shape
    for i, (_, index) in enumerate(blocks):
        source = pl.ds(pl.multiple_of(index * width, width), width)
        for at, third in enumerate(thirds):
            columns = slice(at * width, (at + 1) * width)
            rows_ref[i * width : (i + 1) * width, columns] = w_ref[third, source, :]

    def step(number, _):
        at = pl.ds(pl.multiple_of(number * CHUNK, CHUNK), CHUNK)
        total = jnp.zeros((CHUNK, width), F32)
        for i, (ref, index) in enumerate(blocks):
            value = ref[at, :].astype(F32)
            total = total + value * value
            gain = gain_ref[pl.ds(index, 1), :]
            scaled_ref[:, i * width : (i + 1) * width] = (value * gain).astype(BF16)
        put(at, total, jnp.dot(scaled_ref[...], rows_ref[...], preferred_element_type=F32))
        return 0

    lax.fori_loop(0, rows // CHUNK, step, 0)


def own_half_kernel(own_ref, gain_ref, w_ref, square_ref, product_ref, *scratch):
    core = lax.axis_index("core")

    def put(at, square, product):
        square_ref[at, :] = square
        product_ref[at, :] = product

    blocks = [(own_ref.at[chip], 2 * chip + core) for chip in range(own_ref.shape[0])]
    block_product(blocks, (0, 1, 2), gain_ref, w_ref, *scratch, put)


def finish(thirds, other_ref, gain_ref, w_ref, square0_ref, product0_ref, scratch, put):
    core = lax.axis_index("core")
    width = gain_ref.shape[1]
    features = gain_ref.shape[0] * width
    columns = slice(thirds[0] * width, (thirds[-1] + 1) * width)

    def add(at, square, product):
        mean = jnp.sum(square0_ref[at, :] + square, axis=-1, keepdims=True) / features
        factor = lax.rsqrt(mean + 1e-05)
        put(at, ((product0_ref[at, columns] + product) * factor).astype(BF16))

    blocks = [(other_ref.at[chip], 2 * chip + 1 - core) for chip in range(other_ref.shape[0])]
    block_product(blocks, thirds, gain_ref, w_ref, *scratch, add)


def kv_kernel(other_ref, gain_ref, w_ref, square0_ref, product0_ref, kv_ref, *scratch):
    rows, width = square0_ref.shape

    def put(at, both):
        kv_ref[at, :] = both[:, :width]
        kv_ref[pl.ds(pl.multiple_of(rows + at.start, CHUNK), CHUNK), :] = both[:, width:]

    finish((1, 2), other_ref, gain_ref, w_ref, square0_ref, product0_ref, scratch, put)


def q_kernel(other_ref, gain_ref, w_ref, square0_ref, product0_ref, q_ref, *scratch):
    def put(at, queries):
        q_ref[at, :] = queries

    finish((0,), other_ref, gain_ref, w_ref, square0_ref, product0_ref, scratch, put)


def attend_block(q_ref, kv_ref, seen, before, put):
    rows, width = q_ref.shape
    chunk = 256
    heads = width // HEAD_DIM
    lane = lax.broadcasted_iota(jnp.int32, (1, width), 1)
    keys = kv_ref[pl.ds(0, rows), :]
    values = kv_ref[pl.ds(rows, rows), :]
    summed = []
    for head in range(heads):
        mine = lane // HEAD_DIM == head
        ones = jnp.broadcast_to(jnp.where(mine, 1.0, 0.0), values.shape).astype(BF16)
        summed.append(jnp.concatenate([jnp.where(mine, values, 0).astype(BF16), ones], axis=1))
    for start in range(0, rows, chunk):
        at = pl.ds(start, chunk)
        queries = q_ref[at, :] * HEAD_DIM ** (-0.5)
        if before is not None:
            tops = before[0][at, :]
        new_tops = jnp.zeros((chunk, width), F32)
        gained = jnp.zeros((chunk, 2 * width), F32)
        for head in range(heads):
            mine = lane // HEAD_DIM == head
            scores = lax.dot_general(
                jnp.where(mine, queries, 0).astype(BF16),
                keys,
                (((1,), (1,)), ((), ())),
                preferred_element_type=F32,
            )
            if seen is not None:
                scores = jnp.where(seen, scores, -1e30)
            top = jnp.max(scores, axis=-1, keepdims=True)
            if before is not None:
                top = jnp.maximum(top, tops[:, head * HEAD_DIM : head * HEAD_DIM + 1])
            expd = jnp.exp(scores - top).astype(BF16)
            gained = gained + jnp.dot(expd, summed[head], preferred_element_type=F32)
            new_tops = jnp.where(mine, top, new_tops)
        mixed, total = gained[:, :width], gained[:, width:]
        if before is not None:
            shrink = jnp.exp(tops - new_tops)
            mixed = before[2][at, :] * shrink + mixed
            total = before[1][at, :] * shrink + total
        put(at, new_tops, total, mixed)


def is_seen(turn, mask_ref):
    odd = (lax.axis_index("region") + lax.axis_index("core")) & 1
    offset = (1, -1, -2, 2)[turn]
    wanted = jnp.where(odd == 0, OFFSETS.index(offset), OFFSETS.index(-offset))
    mask = mask_ref[...]
    lane = lax.broadcasted_iota(jnp.int32, mask.shape, 1)
    return jnp.sum(jnp.where(lane == wanted, mask, 0), axis=-1, keepdims=True) > 0


def own_kernel(q_ref, kv_ref, *states):
    def put(at, *values):
        for ref, value in zip(states, values):
            ref[at, :] = value

    attend_block(q_ref, kv_ref, None, None, put)


def peer_kernel(turn, mask_ref, q_ref, kv_ref, *states):
    def put(at, *values):
        for ref, value in zip(states[3:], values):
            ref[at, :] = value

    attend_block(q_ref, kv_ref, is_seen(turn, mask_ref), states[:3], put)


def last_kernel(turn, mask_ref, q_ref, kv_ref, top_ref, total_ref, mixed_ref, w_ref, out_ref):
    rows, width = q_ref.shape

    def put(at, top, total, mixed):
        out_ref[at, :] = (mixed / total).astype(BF16)

    attend_block(q_ref, kv_ref, is_seen(turn, mask_ref), (top_ref, total_ref, mixed_ref), put)
    part = 1 - lax.axis_index("core")
    for block in range(w_ref.shape[1] // (2 * width)):
        at = pl.ds(pl.multiple_of((2 * block + part) * width, width), width)
        out_ref[rows + block * width : rows + (block + 1) * width, :] = w_ref[:, at]


def share_kernel(chip_ref, w_ref, out_ref):
    blocks, rows, width = out_ref.shape
    core = lax.axis_index("core")
    both = jnp.concatenate([chip_ref[core, :rows, :], chip_ref[1 - core, :rows, :]], axis=1)
    for block in range(blocks):
        at = pl.ds(pl.multiple_of((2 * block + core) * width, width), width)
        w_other = chip_ref[1 - core, rows + block * width : rows + (block + 1) * width, :]
        weight = jnp.concatenate([w_ref[:, at], w_other], axis=0)
        out_ref[block] = jnp.dot(both, weight, preferred_element_type=F32).astype(BF16)


def sum_kernel(base_ref, parts_ref, state_ref, back_ref):
    total = base_ref[...].astype(F32)
    for block in range(parts_ref.shape[0]):
        total = total + parts_ref[block].astype(F32)
    state_ref[...] = total
    back_ref[...] = total.astype(BF16)


def hot_kernel(slot_ref, hot_ref):
    lanes, slots = slot_ref.shape[1], hot_ref.shape[1]
    number = lax.broadcasted_iota(jnp.int32, (lanes, slots), 1)
    for i in range(slot_ref.shape[0]):
        down = jnp.broadcast_to(slot_ref[i : i + 1, :], (lanes, lanes)).T
        wanted = jnp.concatenate([down] * (slots // lanes), axis=1)
        hot_ref[i * lanes : (i + 1) * lanes, :] = jnp.where(number == wanted, 1.0, 0.0).astype(BF16)


def decode_kernel(hot_ref, returned_ref, grid_ref, out_ref, part_ref, sems):
    parts, rows, _ = part_ref.shape
    copies = []
    for i in range(parts):
        at = pl.ds(i * rows, rows)
        back = jnp.dot(hot_ref[at, :], returned_ref[...], preferred_element_type=F32)
        part_ref[i] = (grid_ref[at, :].astype(F32) + back).astype(BF16)
        copies.append(pltpu.make_async_copy(part_ref.at[i], out_ref.at[at], sems.at[i]))
        copies[i].start()
    for copy in copies:
        copy.wait()


def call(kernel, outs, name, scratch=(), flops=0, bytes_accessed=0, transcendentals=0):
    def run(*args):
        return pl.pallas_call(
            kernel,
            out_shape=outs,
            in_specs=[VMEM] * len(args),
            out_specs=jax.tree.map(lambda _: VMEM, outs),
            scratch_shapes=list(scratch),
            compiler_params=PARAMS,
            name=name,
            cost_estimate=pl.CostEstimate(
                flops=flops, bytes_accessed=bytes_accessed, transcendentals=transcendentals
            ),
        )(*args)

    return run


def on_device(grid, g2m_weight, g2m_slot, slot_node, peer_mask, norm_gain, w_qkv, w_out):
    regions = lax.axis_size("region")
    chips = lax.axis_size("x")
    parts = chips * lax.axis_size("core")
    cap = slot_node.shape[2]
    slots = regions * cap
    rows = slots
    width = grid.shape[1]
    low = jax.ShapeDtypeStruct((rows, width), BF16)
    state = jax.ShapeDtypeStruct((rows, width), F32)

    scaled = (g2m_weight[:, None] * grid.astype(F32)).astype(BF16)
    slot_hot = (g2m_slot[None, :] == jnp.arange(slots, dtype=jnp.int32)[:, None]).astype(BF16)
    partial_value = jnp.dot(slot_hot, scaled, preferred_element_type=F32).astype(BF16)
    mesh_low = exchange(partial_value.reshape(regions, cap, width), "region").reshape(rows, width)

    own = exchange(jnp.broadcast_to(mesh_low, (chips, rows, width)), "x")
    other = other_core(own)
    gain = norm_gain.reshape(parts, width)

    def product(kernel, outs, name, thirds, *args):
        depth = chips * width
        return call(
            kernel,
            outs,
            name,
            scratch=[pltpu.VMEM((CHUNK, depth), BF16), pltpu.VMEM((depth, thirds * width), BF16)],
            flops=2 * thirds * rows * depth * width,
            bytes_accessed=2 << 20,
        )(*args)

    sums = (state, jax.ShapeDtypeStruct((rows, 3 * width), F32))
    kvs = jax.ShapeDtypeStruct((2 * rows, width), BF16)
    so_far = product(own_half_kernel, sums, "own_half", 3, own, gain, w_qkv)
    kv = product(kv_kernel, kvs, "kv", 2, other, gain, w_qkv, *so_far)
    queries = product(q_kernel, low, "q", 1, other, gain, w_qkv, *so_far)

    cost = dict(flops=8 * rows * rows * width, transcendentals=2 * rows * rows)

    def attend(turn, *args):
        lasts = jax.ShapeDtypeStruct((rows + chips * width, width), BF16)
        outs, kernel = (lasts, last_kernel) if turn == 3 else ((state,) * 3, peer_kernel)
        return call(lambda *refs: kernel(turn, *refs), outs, f"peer{turn}", **cost)(
            peer_mask, queries, *args
        )

    kv0 = swapped(kv, "region", True)
    kv1 = swapped(kv, "region", False)
    so_far = call(own_kernel, (state,) * 3, "own", **cost)(queries, kv)
    kv2 = swapped(after(kv0, so_far[0]), "region", False)
    kv3 = swapped(kv1, "region", True)
    so_far = attend(0, kv0, *so_far)
    so_far = attend(1, kv1, *so_far)
    so_far = attend(2, kv2, *so_far)
    attended = attend(3, kv3, *so_far, w_out)

    summed = call(
        share_kernel,
        jax.ShapeDtypeStruct((chips, rows, width), BF16),
        "share",
        flops=4 * rows * width * chips * width,
    )(lax.all_gather(attended, "core"), w_out)
    mesh_slots, mesh_back = call(sum_kernel, (state, low), "sum", bytes_accessed=1 << 20)(
        mesh_low, exchange(summed, "x")
    )

    returned = exchange(mesh_back.reshape(regions, cap, width), "region").reshape(slots, width)
    flat_nodes = slot_node[0].reshape(-1)
    node_hot = (jnp.arange(rows, dtype=jnp.int32)[:, None] == flat_nodes[None, :]).astype(F32)
    mesh_state = jnp.dot(
        node_hot, mesh_slots, precision=lax.Precision.HIGHEST, preferred_element_type=F32
    )
    hots = jax.ShapeDtypeStruct((grid.shape[0], slots), BF16)
    slot_rows = after(g2m_slot.reshape(-1, width), mesh_back)
    hot = call(hot_kernel, hots, "hot", bytes_accessed=1 << 21)(slot_rows)
    grid_out = pl.pallas_call(
        decode_kernel,
        out_shape=jax.ShapeDtypeStruct(grid.shape, BF16),
        in_specs=[VMEM] * 3,
        out_specs=pl.BlockSpec(memory_space=pl.ANY),
        scratch_shapes=[
            pltpu.VMEM((4, grid.shape[0] // 4, width), BF16),
            pltpu.SemaphoreType.DMA((4,)),
        ],
        compiler_params=PARAMS,
        name="decode",
    )(hot, returned, grid)
    return (mesh_state, grid_out)


def solution(mesh):
    regions, model = mesh.devices.shape
    split = Mesh(mesh.devices.reshape(regions, model // 2, 2), ("region", "x", "core"))
    model = ("x", "core")
    return jax.shard_map(
        on_device,
        mesh=split,
        in_specs=(
            P("region", model),
            P("region"),
            P("region"),
            P("region", None, None),
            P("region", None),
            P(),
            P(None, None, model),
            P(model, None),
        ),
        out_specs=(P("region", model), P("region", model)),
        check_vma=False,
    )
```
